32 devices in a mesh: groups: 2 (over y), graph: 4 (over z), dp: 4 (over x, core).
Axes of the slice: x: 2, y: 2, z: 4, core: 2. Of those that a mesh axis runs over, the one named last changes fastest.
Arguments:
- node_feats: bfloat16 [8, 192, 9, 512], P(('groups', 'dp'), 'graph'), parts along dimension 0, may hold values from -6 to 6
- frac_pos: float32 [8, 3, 192], P(('groups', 'dp'), None, 'graph'), parts along dimension 0, may hold values from 0 to 1
- lattice: float32 [8, 3, 3], P(('groups', 'dp')), parts along dimension 0, may hold values from -1 to 10, as said below
- edge_count: int32 [8, 4], P(('groups', 'dp'), 'graph'), parts along dimension 0, may hold values from 32 to 256, as said below
- edge_target: int32 [8, 1024], P(('groups', 'dp'), 'graph'), parts along dimension 0, may hold values from 0 to 47
- edge_source: int32 [8, 1024], P(('groups', 'dp'), 'graph'), parts along dimension 0, may hold values from 0 to 191, as said below
- edge_shift: int32 [8, 3, 1024], P(('groups', 'dp'), None, 'graph'), parts along dimension 0, may hold values from -1 to 1
- cotangent: bfloat16 [8, 192, 9, 512], P(('groups', 'dp'), 'graph'), parts along dimension 0, may hold values from -6 to 6
- w_in: bfloat16 [512, 512], P('dp'), may hold values from -0.25 to 0.25
- w_out: bfloat16 [512, 512], P('dp'), may hold values from -0.25 to 0.25
- w_rad: bfloat16 [128, 1536], P('dp'), may hold values from -3 to 3
Outputs:
- new_feats: bfloat16 [8, 192, 9, 512], P(('groups', 'dp'), 'graph'), parts along dimension 0
- grad_feats: bfloat16 [8, 192, 9, 512], P(('groups', 'dp'), 'graph'), parts along dimension 0
- grad_w_in: float32 [1024, 512], P(('groups', 'dp')), parts along dimension 0
- grad_w_out: float32 [1024, 512], P(('groups', 'dp')), parts along dimension 0
- grad_w_rad: float32 [256, 1536], P(('groups', 'dp')), parts along dimension 0
The draws below stay inside these ranges and needn't reach their ends.
There are 2 independent parts, one for each index of `groups`. The reference program is written for one: setup_inputs(seed, part) draws one part's arguments, and reference() takes and returns one part's arrays. A program takes and returns all parts, laid end to end along the dimension named above; an argument that names none is the same for every part. Nothing has to cross between parts.
Inputs may be any that keep to these rules, and one draw needn't show every extreme that they name: `edge_count`: in every cell exactly one device has all 256 slots live; the others have 256 // 8 to 128 live slots, always its first ones. `edge_source`: the source of an edge slot of device block g is an atom of g's own block or one of the 16 atoms just before or just after it, counted cyclically over the cell's atoms; on every device some edge takes the first and some the last of these atoms. `lattice`: diagonal entries lie in 8 to 10, the others in -1 to 1.
All inputs are finite; a program needn't handle non-finite values.
Results may differ from the reference program's by a relative error of at most 0.014.
Values may be sent and summed in bfloat16 or wider, within the bound.
A program may use at most 64 MiB of HBM per device.

```python
import math
import jax
import jax.numpy as jnp
from jax import lax

C = 512
COMPS = 9
RB = 128
ATOM_DEV = 48
EDGE_DEV = 256
RIM = 16
CELLS = 4
RANKS = 4
ATOMS = 192
EDGES = 1024


def draw_lattice(key, part):
    key = jax.random.fold_in(key, 11)
    diag_key, off_key = jax.random.split(key)
    diagonal = jax.random.uniform(diag_key, (CELLS, 3), jnp.float32, 8.0, 10.0)
    offdiag = jax.random.uniform(off_key, (CELLS, 3, 3), jnp.float32, -1.0, 1.0)
    eye_mask = jnp.eye(3, dtype=jnp.float32)
    return offdiag * (1.0 - eye_mask) + diagonal[:, :, None] * eye_mask


def draw_edge_count(key, part):
    key = jax.random.fold_in(key, 12)
    base_key, full_key = jax.random.split(key)
    base_count = jax.random.randint(base_key, (CELLS, RANKS), EDGE_DEV // 8, EDGE_DEV // 2 + 1, dtype=jnp.int32)
    busiest = jax.random.randint(full_key, (CELLS, 1), 0, RANKS, dtype=jnp.int32)
    column = jnp.arange(RANKS, dtype=jnp.int32)[None, :]
    return jnp.where(column == busiest, EDGE_DEV, base_count).astype(jnp.int32)


def draw_edge_source(key, part):
    key = jax.random.fold_in(key, 13)
    offset = jax.random.randint(key, (CELLS, EDGES), -RIM, ATOM_DEV + RIM, dtype=jnp.int32)
    slot_ids = jnp.arange(EDGES, dtype=jnp.int32) % EDGE_DEV
    offset = jnp.where(slot_ids[None, :] == 0, -RIM, jnp.where(slot_ids[None, :] == 1, ATOM_DEV + RIM - 1, offset))
    owner_rank = jnp.arange(EDGES, dtype=jnp.int32) // EDGE_DEV
    return jnp.mod(owner_rank[None, :] * ATOM_DEV + offset, ATOMS).astype(jnp.int32)


def set_ends(array, key, smallest, top_value):
    shape = array.shape
    index_at = [jax.random.randint(jax.random.fold_in(key, axis), (), 0, shape[axis]) for axis in range(len(shape))]
    array = array.at[tuple(index_at)].set(smallest)
    longest = shape.index(max(shape))
    index_at[longest] = (index_at[longest] + 1) % shape[longest]
    return array.at[tuple(index_at)].set(top_value)


def levels(key, extent, cuts, least, largest):
    loudness = 1.0
    for position, shards_of in cuts:
        heights = jax.random.uniform(jax.random.fold_in(jax.random.fold_in(key, 6), position), (shards_of,), jnp.float32, least / len(cuts), largest / len(cuts))
        loudness = loudness * jnp.repeat(jnp.exp(heights), extent[position] // shards_of).reshape((-1,) + (1,) * (len(extent) - 1 - position))
    return loudness


def scatter_about(key, shape, scale, reach, pieces=(), kind=jnp.bfloat16):
    result = jax.random.normal(key, shape, jnp.float32) * scale
    if len(pieces) > 0:
        result = levels(key, shape, pieces, -0.22, 0.18) * result
    return jnp.clip(result, min=-reach, max=reach).astype(kind)


def setup_inputs(seed: int = 0, part: int = 0) -> dict:
    key_of = jax.random.split(jax.random.key(seed), 12)
    own_keys = jax.random.split(jax.random.fold_in(key_of[11], part), 12)
    return {
        "node_feats": scatter_about(own_keys[0], (CELLS, ATOMS, COMPS, C), 1.0, 6.0, ((0, 4), (1, 4))),
        "frac_pos": jnp.clip(1.0 * jax.random.uniform(own_keys[1], (CELLS, 3, ATOMS), jnp.float32) ** levels(own_keys[1], (CELLS, 3, ATOMS), ((0, 4), (2, 4)), -0.2, 0.2), 0.0, 1.0),
        "lattice": draw_lattice(jax.random.fold_in(jax.random.fold_in(key_of[11], part), 71), part),
        "edge_count": draw_edge_count(jax.random.fold_in(jax.random.fold_in(key_of[11], part), 71), part),
        "edge_target": set_ends(jax.random.randint(own_keys[4], (CELLS, EDGES), 0, ATOM_DEV), jax.random.fold_in(own_keys[4], 1), 0, ATOM_DEV - 1).astype(jnp.int32),
        "edge_source": draw_edge_source(jax.random.fold_in(jax.random.fold_in(key_of[11], part), 71), part),
        "edge_shift": set_ends(jax.random.randint(own_keys[6], (CELLS, 3, EDGES), -1, 2), jax.random.fold_in(own_keys[6], 1), -1, 1).astype(jnp.int32),
        "cotangent": scatter_about(own_keys[7], (CELLS, ATOMS, COMPS, C), 1.0, 6.0, ((0, 4), (1, 4))),
        "w_in": scatter_about(key_of[8], (C, C), C ** -0.5, 0.25, ((0, 4),)),
        "w_out": scatter_about(key_of[9], (C, C), C ** -0.5, 0.25, ((0, 4),)),
        "w_rad": scatter_about(key_of[10], (RB, 3 * C), 4 ** -0.5, 3.0, ((0, 4),)),
    }


CUTOFF = 48.0
ROOT_THREE = math.sqrt(3.0)
ROOT_FIVE = math.sqrt(5.0)
ROOT_FIFTEEN = math.sqrt(15.0)

def geometry(frac_src, frac_tgt, image_shift, lattice_rows, live_mask):
    frac_diff = frac_src + image_shift.astype(jnp.float32) - frac_tgt
    displace = frac_diff[0][None, :] * lattice_rows[0][:, None] + frac_diff[1][None, :] * lattice_rows[1][:, None] + frac_diff[2][None, :] * lattice_rows[2][:, None]
    distance = jnp.sqrt(lax.optimization_barrier(jnp.sum(displace * displace, axis=0)) + 1.0)
    unit_x = displace[0] / distance
    unit_y = displace[1] / distance
    unit_z = displace[2] / distance
    harm_one = ROOT_THREE * jnp.stack([unit_y, unit_z, unit_x], axis=1)
    harm_two = jnp.stack([ROOT_FIFTEEN * unit_x * unit_y, ROOT_FIFTEEN * unit_y * unit_z, 0.5 * ROOT_FIVE * (2.0 * unit_z * unit_z - unit_x * unit_x - unit_y * unit_y), ROOT_FIFTEEN * unit_x * unit_z, 0.5 * ROOT_FIFTEEN * (unit_x * unit_x - unit_y * unit_y)], axis=1)
    centres = CUTOFF * jnp.arange(RB, dtype=jnp.float32) / (RB - 1)
    spread = 2.0 * CUTOFF / RB
    envelope = 0.5 * (jnp.cos(math.pi * distance / CUTOFF) + 1.0) * live_mask.astype(jnp.float32)
    radial_basis = (jnp.exp(-jnp.square((distance[:, None] - centres[None, :]) / spread)) * envelope[:, None]).astype(jnp.bfloat16)
    return (radial_basis, harm_one, harm_two)

def split_gates(src_rows, radial_gates, harm_one, harm_two):
    channels = src_rows.shape[2]
    src_float = src_rows.astype(jnp.float32)
    scalars = src_float[:, 0, :]
    gate_zero = radial_gates[:, :channels]
    gate_one = radial_gates[:, channels:2 * channels]
    gate_two = radial_gates[:, 2 * channels:]
    inner_one = harm_one[:, :, None] * scalars[:, None, :] + src_float[:, 1:4, :]
    inner_two = harm_two[:, :, None] * scalars[:, None, :] + src_float[:, 4:9, :]
    return (scalars, gate_zero, gate_one, gate_two, inner_one, inner_two)

def messages(src_rows, radial_gates, harm_one, harm_two):
    scalars, gate_zero, gate_one, gate_two, inner_one, inner_two = split_gates(src_rows, radial_gates, harm_one, harm_two)
    return jnp.concatenate([(gate_zero * scalars)[:, None, :], gate_one[:, None, :] * inner_one, gate_two[:, None, :] * inner_two], axis=1)

def message_grads(src_rows, radial_gates, harm_one, harm_two, d_msgs):
    scalars, gate_zero, gate_one, gate_two, inner_one, inner_two = split_gates(src_rows, radial_gates, harm_one, harm_two)
    d_zero = d_msgs[:, 0, :]
    d_one = d_msgs[:, 1:4, :]
    d_two = d_msgs[:, 4:9, :]
    d_gates = jnp.concatenate([d_zero * scalars, lax.optimization_barrier(jnp.sum(d_one * inner_one, axis=1)), lax.optimization_barrier(jnp.sum(d_two * inner_two, axis=1))], axis=1)
    d_scalars = d_zero * gate_zero + gate_one * lax.optimization_barrier(jnp.sum(d_one * harm_one[:, :, None], axis=1)) + gate_two * lax.optimization_barrier(jnp.sum(d_two * harm_two[:, :, None], axis=1))
    d_rows = jnp.concatenate([d_scalars[:, None, :], gate_one[:, None, :] * d_one, gate_two[:, None, :] * d_two], axis=1)
    return (d_gates, d_rows)

def gated_output(features, summed_b, w_out, cotangent):
    atom_count, comp_count, channels = features.shape
    pre_gate = jnp.dot(summed_b.reshape(-1, channels), w_out, preferred_element_type=jnp.float32).reshape(atom_count, comp_count, channels)
    gate_value = jax.nn.sigmoid(pre_gate[:, 0, :])
    new_feats = (features.astype(jnp.float32) + pre_gate * gate_value[:, None, :]).astype(jnp.bfloat16)
    upstream = cotangent.astype(jnp.float32)
    gate_slope = gate_value * (1.0 - gate_value)
    d_zero = upstream[:, 0, :] * gate_value + gate_slope * lax.optimization_barrier(jnp.sum(upstream * pre_gate, axis=1))
    d_pregate = jnp.concatenate([d_zero[:, None, :], upstream[:, 1:, :] * gate_value[:, None, :]], axis=1).astype(jnp.bfloat16)
    return (new_feats, d_pregate)

def cell_terms(features, fractions, lattice_rows, counts, targets, sources, shifts, cotangent, w_in, w_out, w_rad):
    atom_count, comp_count, channels = features.shape
    projected = jnp.dot(features.reshape(-1, channels), w_in, preferred_element_type=jnp.float32)
    projected = projected.astype(jnp.bfloat16).reshape(atom_count, comp_count, channels)

    def group_edges(group_id):
        first_edge = group_id * EDGE_DEV
        tgt_ids = lax.dynamic_slice_in_dim(targets, first_edge, EDGE_DEV) + group_id * ATOM_DEV
        src_ids = lax.dynamic_slice_in_dim(sources, first_edge, EDGE_DEV)
        image_shift = lax.dynamic_slice_in_dim(shifts, first_edge, EDGE_DEV, 1)
        live_mask = jnp.arange(EDGE_DEV, dtype=jnp.int32) < counts[group_id]
        radial_basis, harm_one, harm_two = geometry(fractions[:, src_ids], fractions[:, tgt_ids], image_shift, lattice_rows, live_mask)
        radial_gates = jnp.dot(radial_basis, w_rad, preferred_element_type=jnp.float32)
        return (tgt_ids, src_ids, radial_basis, harm_one, harm_two, radial_gates, projected[src_ids])

    def forward_step(summed, group_id):
        tgt_ids, src_ids, radial_basis, harm_one, harm_two, radial_gates, src_rows = group_edges(group_id)
        return (summed.at[tgt_ids].add(messages(src_rows, radial_gates, harm_one, harm_two)), None)
    group_list = jnp.arange(RANKS, dtype=jnp.int32)
    summed, unused = lax.scan(forward_step, jnp.zeros((atom_count, comp_count, channels), jnp.float32), group_list)
    summed_b = (0.25 * summed).astype(jnp.bfloat16)
    new_feats, d_pregate = gated_output(features, summed_b, w_out, cotangent)
    d_summed = jnp.dot(d_pregate.reshape(-1, channels), w_out.T, preferred_element_type=jnp.float32).reshape(atom_count, comp_count, channels)

    def backward_step(state_pair, group_id):
        d_proj, grad_rad = state_pair
        tgt_ids, src_ids, radial_basis, harm_one, harm_two, radial_gates, src_rows = group_edges(group_id)
        d_gates, d_rows = message_grads(src_rows, radial_gates, harm_one, harm_two, 0.25 * d_summed[tgt_ids])
        grad_rad = grad_rad + jnp.dot(radial_basis.T, d_gates.astype(jnp.bfloat16), preferred_element_type=jnp.float32)
        return ((d_proj.at[src_ids].add(d_rows), grad_rad), None)
    start_pair = (jnp.zeros((atom_count, comp_count, channels), jnp.float32), jnp.zeros((RB, 3 * channels), jnp.float32))
    (d_proj, grad_rad), unused = lax.scan(backward_step, start_pair, group_list)
    d_proj_b = d_proj.astype(jnp.bfloat16).reshape(-1, channels)
    grad_in = jnp.dot(features.reshape(-1, channels).T, d_proj_b, preferred_element_type=jnp.float32)
    grad_out = jnp.dot(summed_b.reshape(-1, channels).T, d_pregate.reshape(-1, channels), preferred_element_type=jnp.float32)
    back = jnp.dot(d_proj_b, w_in.T, preferred_element_type=jnp.float32).reshape(atom_count, comp_count, channels)
    grad_feats = (cotangent.astype(jnp.float32) + back).astype(jnp.bfloat16)
    return (new_feats, grad_feats, grad_in, grad_out, grad_rad)

def reference(node_feats, frac_pos, lattice, edge_count, edge_target, edge_source, edge_shift, cotangent, w_in, w_out, w_rad):

    def one_cell(cell_args):
        return cell_terms(cell_args[0], cell_args[1], cell_args[2], cell_args[3], cell_args[4], cell_args[5], cell_args[6], cell_args[7], w_in, w_out, w_rad)
    results = lax.map(one_cell, (node_feats, frac_pos, lattice, edge_count, edge_target, edge_source, edge_shift, cotangent))
    grad_scale = 1.0 / ATOMS
    return (results[0], results[1], grad_scale * lax.optimization_barrier(jnp.sum(results[2], axis=0)), grad_scale * lax.optimization_barrier(jnp.sum(results[3], axis=0)), grad_scale * lax.optimization_barrier(jnp.sum(results[4], axis=0)))
```

```python
import functools
import math

import jax
import jax.numpy as jnp
from jax import lax
from jax.experimental import pallas as pl
from jax.experimental.pallas import tpu as pltpu
from jax.sharding import PartitionSpec as P

RB = 128
RIM = 16
EDGE_ROWS = 16
CUTOFF = 48.0
ROOT_THREE = math.sqrt(3.0)
ROOT_FIVE = math.sqrt(5.0)
ROOT_FIFTEEN = math.sqrt(15.0)
MESH = pl.DeviceIdType.MESH
F32 = jnp.float32
BF16 = jnp.bfloat16


def dot(a, b, dims=((1,), (0,))):
    return lax.dot_general(a, b, (dims, ((), ())), preferred_element_type=F32)


def log2(value):
    bits = value.bit_length() - 1
    assert 1 << bits == value
    return bits


class Reduction:
    def __init__(self, place, bufs, sems, out_ref):
        self.place = place
        self.part, self.ra, self.sb, self.rb, self.sc, self.rc, self.rd = bufs
        self.a_s, self.a_r, self.b_s, self.b_r, self.c_s, self.c_r, self.d_s, self.d_r = sems
        self.out_ref = out_ref
        self.sends = []
        self.split = self.rd.shape[1] != self.out_ref.shape[0]

    def send(self, src, dst, send_sem, recv_sem, where):
        copy = pltpu.make_async_remote_copy(
            src_ref=src, dst_ref=dst, send_sem=send_sem, recv_sem=recv_sem,
            device_id=where, device_id_type=MESH,
        )
        copy.start()
        self.sends.append(copy)

    def arrived(self, dst, send_sem, recv_sem, where):
        pltpu.make_async_remote_copy(
            src_ref=dst, dst_ref=dst, send_sem=send_sem, recv_sem=recv_sem,
            device_id=where, device_id_type=MESH,
        ).wait_recv()

    def put(self, value):
        x_count, n = self.part.shape[1], self.part.shape[2]
        for r in range(2 * x_count):
            self.part[r % 2, r // 2] = value[r * n : (r + 1) * n].astype(BF16)

    def stage_a(self):
        core, peer = self.place["core"], self.place["peer"]
        self.send(self.part.at[1 - core], self.ra, self.a_s, self.a_r, {"dp": peer})

    def stage_b(self):
        core, peer, x, xs = (self.place[k] for k in ("core", "peer", "x", "x_count"))
        self.arrived(self.ra, self.a_s, self.a_r, {"dp": peer})
        for i in range(xs):
            self.sb[i] = (self.part.at[core, i][...].astype(F32) + self.ra[i].astype(F32)).astype(BF16)
        for j in range(1, xs):
            to = lax.rem(x + j, xs)
            self.send(self.sb.at[to], self.rb.at[x], self.b_s.at[j], self.b_r.at[x], {"dp": 2 * to + core})

    def stage_c(self):
        core, x, xs, z, zs = (self.place[k] for k in ("core", "x", "x_count", "z", "z_count"))
        total = self.sb.at[x][...].astype(F32)
        for j in range(1, xs):
            frm = lax.rem(x + xs - j, xs)
            self.arrived(self.rb.at[frm], self.b_s.at[j], self.b_r.at[frm], {"dp": 2 * frm + core})
            total = total + self.rb.at[frm][...].astype(F32)
        if self.split:
            self.sc[...] = total.astype(BF16).reshape(self.sc.shape)
            for j in range(1, zs):
                to = lax.rem(z + j, zs)
                self.send(self.sc.at[to], self.rc.at[z], self.c_s.at[j], self.c_r.at[z], {"graph": to})
        else:
            self.rd.at[z][...] = total.astype(BF16)
            self.spread()

    def spread(self):
        z, zs = self.place["z"], self.place["z_count"]
        for j in range(1, zs):
            to = lax.rem(z + j, zs)
            self.send(self.rd.at[z], self.rd.at[z], self.d_s.at[j], self.d_r.at[z], {"graph": to})

    def stage_d(self):
        z, zs = self.place["z"], self.place["z_count"]
        if self.split:
            total = self.sc.at[z][...].astype(F32)
            for j in range(1, zs):
                frm = lax.rem(z + zs - j, zs)
                self.arrived(self.rc.at[frm], self.c_s.at[j], self.c_r.at[frm], {"graph": frm})
                total = total + self.rc.at[frm][...].astype(F32)
            self.rd.at[z][...] = total.astype(BF16)
            self.spread()

    def finish(self):
        z, zs = self.place["z"], self.place["z_count"]
        for j in range(1, zs):
            frm = lax.rem(z + zs - j, zs)
            self.arrived(self.rd.at[frm], self.d_s.at[j], self.d_r.at[frm], {"graph": frm})
        if self.split:
            self.out_ref[...] = self.rd[...].reshape(self.out_ref.shape)
        else:
            total = self.rd[0].astype(F32)
            for i in range(1, zs):
                total = total + self.rd[i].astype(F32)
            self.out_ref[...] = total.astype(BF16)


def kernel(
    x_count, z_count,
    feat_ref, cot_ref, geo_ref, frac_ref, win_ref, wout_ref, wrad_ref,
    new_ref, gf_ref, gin_ref, gout_ref, grad_ref,
    full_in, full_out, full_rad, feat_pad, frac_pad, proj, rows_e, msg_e, dmsg_e, gates, dgates,
    table, columns, basis_l, basis_r, pre, summed_s, dpre_s, dsum_s, d_pad, rim_lo, rim_hi, dproj_s,
    w_send, w_recv, h_send, h_recv, *red_scratch,
):
    comps, atoms, channels = feat_ref.shape
    edges = geo_ref.shape[1]
    padded = atoms + 2 * RIM
    z = lax.axis_index("graph")
    d = lax.axis_index("dp")
    x, core = lax.div(d, 2), lax.rem(d, 2)
    peer = 2 * x + 1 - core
    place = dict(core=core, peer=peer, x=x, x_count=x_count, z=z, z_count=z_count)
    sends = []

    barrier = pltpu.get_barrier_semaphore()
    for j in range(1, z_count):
        pl.semaphore_signal(barrier, inc=1, device_id={"graph": lax.rem(z + j, z_count)}, device_id_type=MESH)
    for j in range(1, x_count):
        pl.semaphore_signal(
            barrier, inc=1, device_id={"dp": 2 * lax.rem(x + j, x_count) + core}, device_id_type=MESH
        )
    pl.semaphore_signal(barrier, inc=1, device_id={"dp": peer}, device_id_type=MESH)
    pl.semaphore_wait(barrier, z_count - 1 + x_count)

    def remote(src, dst, send_sem, recv_sem, where):
        return pltpu.make_async_remote_copy(
            src_ref=src, dst_ref=dst, send_sem=send_sem, recv_sem=recv_sem,
            device_id=where, device_id_type=MESH,
        )

    def send(*args):
        copy = remote(*args)
        copy.start()
        sends.append(copy)

    def gather_start(i, w_ref, full):
        for j in range(1, x_count):
            to = 2 * lax.rem(x + j, x_count) + core
            send(w_ref, full.at[d], w_send.at[i, j], w_recv.at[i, d], {"dp": to})
        send(w_ref, full.at[d], w_send.at[i, 0], w_recv.at[i, d], {"dp": peer})
        full.at[d][...] = w_ref[...]

    def gather_forward(i, full):
        for j in range(1, x_count):
            frm = 2 * lax.rem(x + x_count - j, x_count) + core
            remote(full.at[frm], full.at[frm], w_send.at[i, j], w_recv.at[i, frm], {"dp": frm}).wait_recv()
            send(full.at[frm], full.at[frm], w_send.at[i, x_count + j - 1], w_recv.at[i, frm], {"dp": peer})

    def gather_finish(i, full):
        for j in range(x_count):
            frm = 2 * lax.rem(x + x_count - j, x_count) + 1 - core
            remote(full.at[frm], full.at[frm], w_send.at[i, 0], w_recv.at[i, frm], {"dp": peer}).wait_recv()

    right = {"graph": lax.rem(z + 1, z_count)}
    left = {"graph": lax.rem(z + z_count - 1, z_count)}
    last = atoms - RIM
    ahead = RIM + atoms
    send(frac_ref.at[last:atoms], frac_pad.at[0:RIM], h_send.at[0], h_recv.at[0], right)
    send(frac_ref.at[0:RIM], frac_pad.at[ahead:padded], h_send.at[1], h_recv.at[1], left)
    gather_start(0, win_ref, full_in)
    send(feat_ref.at[:, last:atoms], feat_pad.at[:, 0:RIM], h_send.at[2], h_recv.at[2], right)
    send(feat_ref.at[:, 0:RIM], feat_pad.at[:, ahead:padded], h_send.at[3], h_recv.at[3], left)
    gather_start(1, wrad_ref, full_rad)

    feat_pad[:, RIM:ahead, :] = feat_ref[...]
    frac_pad[RIM:ahead, :] = frac_ref[...]
    remote(frac_pad.at[0:RIM], frac_pad.at[0:RIM], h_send.at[0], h_recv.at[0], left).wait_recv()
    remote(frac_pad.at[ahead:padded], frac_pad.at[ahead:padded], h_send.at[1], h_recv.at[1], right).wait_recv()

    tgt_row = geo_ref[13:14, :]
    src_row = geo_ref[14:15, :]
    hot_src_t = lax.broadcasted_iota(jnp.int32, (padded, edges), 0).astype(F32) == src_row
    hot_tgt_t = lax.broadcasted_iota(jnp.int32, (atoms, edges), 0).astype(F32) == tgt_row
    diffs = []
    for i in range(3):
        f_src = jnp.sum(jnp.where(hot_src_t, frac_pad[:, i : i + 1], 0.0), axis=0, keepdims=True)
        f_tgt = jnp.sum(jnp.where(hot_tgt_t, frac_ref[:, i : i + 1], 0.0), axis=0, keepdims=True)
        diffs.append(f_src + geo_ref[i : i + 1, :] - f_tgt)
    displace = [
        sum(diffs[i] * geo_ref[3 + 3 * i + j : 4 + 3 * i + j, :] for i in range(3)) for j in range(3)
    ]
    distance = jnp.sqrt(
        displace[0] * displace[0] + displace[1] * displace[1] + displace[2] * displace[2] + 1.0
    )
    ux, uy, uz = (displace[j] / distance for j in range(3))
    envelope = 0.5 * (jnp.cos(math.pi * distance / CUTOFF) + 1.0) * geo_ref[12:13, :]
    table[...] = jnp.zeros_like(table)
    entries = [
        envelope,
        ROOT_THREE * uy,
        ROOT_THREE * uz,
        ROOT_THREE * ux,
        ROOT_FIFTEEN * ux * uy,
        ROOT_FIFTEEN * uy * uz,
        0.5 * ROOT_FIVE * (2.0 * uz * uz - ux * ux - uy * uy),
        ROOT_FIFTEEN * ux * uz,
        0.5 * ROOT_FIFTEEN * (ux * ux - uy * uy),
        distance,
        tgt_row,
        src_row,
    ]
    for i, entry in enumerate(entries):
        table[i : i + 1, :] = entry
    columns[...] = table[...].T
    hot_src = (
        lax.broadcasted_iota(jnp.int32, (edges, padded), 1).astype(F32) == columns[:, 11:12]
    ).astype(BF16)
    hot_tgt = (
        lax.broadcasted_iota(jnp.int32, (edges, atoms), 1).astype(F32) == columns[:, 10:11]
    ).astype(BF16)
    hot_src_t = hot_src_t.astype(BF16)
    hot_tgt_t = hot_tgt_t.astype(BF16)

    ranks, rad_rows, rad_cols = full_rad.shape
    quarter = rad_rows // 2
    slot = lax.broadcasted_iota(jnp.int32, (1, 2 * RB), 1)
    half = (slot >> log2(quarter)) & 1
    index = ((slot >> log2(rad_rows)) << log2(quarter)) + (slot & (quarter - 1))
    centres = CUTOFF * index.astype(F32) / (RB - 1)
    offset = (columns[:, 9:10] - centres) / (2.0 * CUTOFF / RB)
    basis = jnp.exp(-(offset * offset)) * columns[:, 0:1]
    basis_l[...] = jnp.where(half == 0, basis, 0.0).astype(BF16)
    basis_r[...] = jnp.where(half == 1, basis, 0.0).astype(BF16)

    gather_forward(0, full_in)
    gather_start(2, wout_ref, full_out)
    gather_forward(1, full_rad)
    gather_finish(0, full_in)
    remote(feat_pad.at[:, 0:RIM], feat_pad.at[:, 0:RIM], h_send.at[2], h_recv.at[2], left).wait_recv()
    remote(feat_pad.at[:, ahead:padded], feat_pad.at[:, ahead:padded], h_send.at[3], h_recv.at[3], right).wait_recv()
    proj[...] = (
        dot(feat_pad[...].reshape(comps * padded, channels), full_in[...].reshape(channels, channels))
        .astype(BF16)
        .reshape(comps, padded, channels)
    )
    for k in range(comps):
        rows_e[k] = dot(hot_src, proj[k]).astype(BF16)
    gather_finish(1, full_rad)
    rad = full_rad[...].reshape(ranks * rad_rows, rad_cols)
    gates[:, :rad_cols] = dot(basis_l[...], rad)
    gates[:, rad_cols:] = dot(basis_r[...], rad)
    gather_forward(2, full_out)

    def gate_of(rows):
        return [gates[rows, i * channels : (i + 1) * channels] for i in range(3)]

    @pl.loop(0, edges // EDGE_ROWS)
    def _(step):
        rows = pl.ds(pl.multiple_of(step * EDGE_ROWS, EDGE_ROWS), EDGE_ROWS)
        harm = columns[rows, :]
        g0, g1, g2 = gate_of(rows)
        scalars = rows_e[0, rows, :].astype(F32)
        msg_e[0, rows, :] = (g0 * scalars).astype(BF16)
        for k in range(1, comps):
            inner = harm[:, k : k + 1] * scalars + rows_e[k, rows, :].astype(F32)
            msg_e[k, rows, :] = ((g1 if k < 4 else g2) * inner).astype(BF16)

    for k in range(comps):
        summed_s[k] = (0.25 * dot(hot_tgt_t, msg_e[k])).astype(BF16)
    gather_finish(2, full_out)
    w_out = full_out[...].reshape(channels, channels)
    flat = (comps * atoms, channels)
    pre[...] = dot(summed_s[...].reshape(flat), w_out).reshape(comps, atoms, channels)

    @pl.loop(0, atoms // 16)
    def _(step):
        rows = pl.ds(pl.multiple_of(step * 16, 16), 16)
        p0 = pre[0, rows, :]
        gate = jax.nn.sigmoid(p0)
        total = jnp.zeros_like(gate)
        for k in range(comps):
            p = pre[k, rows, :]
            u = cot_ref[k, rows, :].astype(F32)
            total = total + u * p
            new_ref[k, rows, :] = (feat_ref[k, rows, :].astype(F32) + p * gate).astype(BF16)
            if k:
                dpre_s[k, rows, :] = (u * gate).astype(BF16)
        u0 = cot_ref[0, rows, :].astype(F32)
        dpre_s[0, rows, :] = (u0 * gate + gate * (1.0 - gate) * total).astype(BF16)

    scale = 1.0 / (z_count * atoms)
    count = len(red_scratch) // 3
    reds = [
        Reduction(place, red_scratch[i * count : i * count + 7], red_scratch[i * count + 7 : (i + 1) * count], out)
        for i, out in enumerate((gout_ref, grad_ref, gin_ref))
    ]
    red_out, red_rad, red_in = reds
    across = ((0,), (0,))
    red_out.put(scale * dot(summed_s[...].reshape(flat), dpre_s[...].reshape(flat), across))
    red_out.stage_a()
    dsum_s[...] = (
        (0.25 * dot(dpre_s[...].reshape(flat), w_out, ((1,), (1,)))).astype(BF16).reshape(comps, atoms, channels)
    )
    red_out.stage_b()
    for k in range(comps):
        dmsg_e[k] = dot(hot_tgt, dsum_s[k]).astype(BF16)

    @pl.loop(0, edges // EDGE_ROWS)
    def _(step):
        rows = pl.ds(pl.multiple_of(step * EDGE_ROWS, EDGE_ROWS), EDGE_ROWS)
        harm = columns[rows, :]
        g0, g1, g2 = gate_of(rows)
        scalars = rows_e[0, rows, :].astype(F32)
        d0 = dmsg_e[0, rows, :].astype(F32)
        dgates[rows, 0:channels] = (d0 * scalars).astype(BF16)
        d_scalars = d0 * g0
        for lo, hi, gate in ((1, 4, g1), (4, 9, g2)):
            mixed = jnp.zeros_like(d0)
            plain = jnp.zeros_like(d0)
            for k in range(lo, hi):
                dk = dmsg_e[k, rows, :].astype(F32)
                mixed = mixed + dk * harm[:, k : k + 1]
                plain = plain + dk * rows_e[k, rows, :].astype(F32)
                msg_e[k, rows, :] = (gate * dk).astype(BF16)
            block = 1 if lo == 1 else 2
            dgates[rows, block * channels : (block + 1) * channels] = (mixed * scalars + plain).astype(BF16)
            d_scalars = d_scalars + gate * mixed
        msg_e[0, rows, :] = d_scalars.astype(BF16)

    red_out.stage_c()
    for k in range(comps):
        d_pad[k] = dot(hot_src_t, msg_e[k]).astype(BF16)
    red_in.put(
        scale
        * dot(
            feat_pad[...].reshape(comps * padded, channels),
            d_pad[...].reshape(comps * padded, channels),
            across,
        )
    )
    red_in.stage_a()
    send(d_pad.at[:, 0:RIM], rim_hi, h_send.at[4], h_recv.at[4], left)
    send(d_pad.at[:, ahead:padded], rim_lo, h_send.at[5], h_recv.at[5], right)
    red_rad.put(
        scale
        * (
            dot(basis_l[...], dgates[:, :rad_cols], across)
            + dot(basis_r[...], dgates[:, rad_cols:], across)
        )
    )
    red_rad.stage_a()
    red_in.stage_b()
    red_rad.stage_b()
    red_out.stage_d()
    red_in.stage_c()
    red_rad.stage_c()
    remote(rim_hi, rim_hi, h_send.at[4], h_recv.at[4], right).wait_recv()
    remote(rim_lo, rim_lo, h_send.at[5], h_recv.at[5], left).wait_recv()
    dproj_s[...] = d_pad[:, RIM:ahead, :]
    dproj_s[:, 0:RIM, :] = (dproj_s[:, 0:RIM, :].astype(F32) + rim_lo[...].astype(F32)).astype(BF16)
    dproj_s[:, last:atoms, :] = (dproj_s[:, last:atoms, :].astype(F32) + rim_hi[...].astype(F32)).astype(BF16)
    red_in.stage_d()
    red_rad.stage_d()
    back = dot(dproj_s[...].reshape(flat), full_in[...].reshape(channels, channels), ((1,), (1,)))
    gf_ref[...] = (
        (cot_ref[...].reshape(flat).astype(F32) + back).astype(BF16).reshape(comps, atoms, channels)
    )
    for red in reds:
        red.finish()
    for red in reds:
        for copy in red.sends:
            copy.wait_send()
    for copy in sends:
        copy.wait_send()


def body(x_count, z_count, node_feats, frac_pos, lattice, edge_count, edge_target, edge_source,
         edge_shift, cotangent, w_in, w_out, w_rad):
    atoms, comps, channels = node_feats.shape[1:]
    edges = edge_target.shape[1]
    padded = atoms + 2 * RIM
    dp = 2 * x_count
    feats = jnp.transpose(node_feats[0], (1, 0, 2))
    cot = jnp.transpose(cotangent[0], (1, 0, 2))
    frac = jnp.pad(frac_pos[0].T, ((0, 0), (0, 125)))
    first = lax.axis_index("graph") * atoms
    local_src = jnp.mod(edge_source[0] - first + RIM, z_count * atoms)
    live = jnp.arange(edges, dtype=jnp.int32) < edge_count[0, 0]
    geo = jnp.concatenate(
        [
            edge_shift[0].astype(F32),
            jnp.broadcast_to(lattice[0].reshape(9, 1), (9, edges)),
            live.astype(F32)[None],
            edge_target[0].astype(F32)[None],
            local_src.astype(F32)[None],
            jnp.zeros((1, edges), F32),
        ],
        axis=0,
    )
    rad_cols = w_rad.shape[1] // 2
    rad = jnp.concatenate([w_rad[:, :rad_cols], w_rad[:, rad_cols:]], axis=0)
    rows, rad_rows = w_in.shape[0], rad.shape[0]

    vmem = lambda shape, dtype=BF16: pltpu.VMEM(shape, dtype)
    dma = pltpu.SemaphoreType.DMA
    scratch = [
        vmem((dp, rows, channels)), vmem((dp, rows, channels)), vmem((dp, rad_rows, rad_cols)),
        vmem((comps, padded, channels)), vmem((padded, 128), F32), vmem((comps, padded, channels)),
        vmem((comps, edges, channels)), vmem((comps, edges, channels)), vmem((comps, edges, channels)),
        vmem((edges, 3 * channels), F32), vmem((edges, 3 * channels)),
        vmem((128, edges), F32), vmem((edges, 128), F32), vmem((edges, 2 * RB)), vmem((edges, 2 * RB)),
        vmem((comps, atoms, channels), F32), vmem((comps, atoms, channels)),
        vmem((comps, atoms, channels)), vmem((comps, atoms, channels)),
        vmem((comps, padded, channels)), vmem((comps, RIM, channels)), vmem((comps, RIM, channels)),
        vmem((comps, atoms, channels)),
        dma((3, 2 * x_count)), dma((3, dp)), dma((6,)), dma((6,)),
    ]
    for n, cols in ((rows, channels), (rad_rows, rad_cols), (rows, channels)):
        piece = n // z_count if n % (16 * z_count) == 0 else n
        scratch += [
            vmem((2, x_count, n, cols)), vmem((x_count, n, cols)), vmem((x_count, n, cols)),
            vmem((x_count, n, cols)), vmem((n // piece, piece, cols)), vmem((z_count, piece, cols)),
            vmem((z_count, piece, cols)),
            dma, dma, dma((x_count,)), dma((x_count,)), dma((z_count,)), dma((z_count,)),
            dma((z_count,)), dma((z_count,)),
        ]
    whole = pl.BlockSpec(memory_space=pltpu.VMEM)
    new, grad_feats, g_in, g_out, g_rad = pl.pallas_call(
        functools.partial(kernel, x_count, z_count),
        out_shape=[
            jax.ShapeDtypeStruct((comps, atoms, channels), BF16),
            jax.ShapeDtypeStruct((comps, atoms, channels), BF16),
            jax.ShapeDtypeStruct((rows, channels), BF16),
            jax.ShapeDtypeStruct((rows, channels), BF16),
            jax.ShapeDtypeStruct((rad_rows, rad_cols), BF16),
        ],
        in_specs=[whole] * 7,
        out_specs=[whole] * 5,
        scratch_shapes=scratch,
        compiler_params=pltpu.CompilerParams(
            collective_id=0, has_side_effects=True, vmem_limit_bytes=50 * 1024 * 1024
        ),
    )(feats, cot, geo, frac, w_in, w_out, rad)
    g_rad = g_rad.astype(F32)
    half = rad_rows // 2
    return (
        jnp.transpose(new, (1, 0, 2))[None],
        jnp.transpose(grad_feats, (1, 0, 2))[None],
        g_in.astype(F32),
        g_out.astype(F32),
        jnp.concatenate([g_rad[:half], g_rad[half:]], axis=1),
    )


def solution(mesh):
    return jax.shard_map(
        functools.partial(body, mesh.shape["dp"] // 2, mesh.shape["graph"]),
        mesh=mesh,
        in_specs=(
            P(("groups", "dp"), "graph", None, None),
            P(("groups", "dp"), None, "graph"),
            P(("groups", "dp"), None, None),
            P(("groups", "dp"), "graph"),
            P(("groups", "dp"), "graph"),
            P(("groups", "dp"), "graph"),
            P(("groups", "dp"), None, "graph"),
            P(("groups", "dp"), "graph", None, None),
            P("dp", None),
            P("dp", None),
            P("dp", None),
        ),
        out_specs=(
            P(("groups", "dp"), "graph", None, None),
            P(("groups", "dp"), "graph", None, None),
            P(("groups", "dp"), None),
            P(("groups", "dp"), None),
            P(("groups", "dp"), None),
        ),
        check_vma=False,
    )
```

```python
import functools
import math

import jax
import jax.numpy as jnp
from jax import lax
from jax.experimental import pallas as pl
from jax.experimental.pallas import tpu as pltpu
from jax.sharding import PartitionSpec as P

RB = 128
RIM = 16
EDGE_ROWS = 16
CUTOFF = 48.0
ROOT_THREE = math.sqrt(3.0)
ROOT_FIVE = math.sqrt(5.0)
ROOT_FIFTEEN = math.sqrt(15.0)
MESH = pl.DeviceIdType.MESH
F32 = jnp.float32
BF16 = jnp.bfloat16


def dot(a, b, dims=((1,), (0,))):
    return lax.dot_general(a, b, (dims, ((), ())), preferred_element_type=F32)


def log2(value):
    bits = value.bit_length() - 1
    assert 1 << bits == value
    return bits


class Reduction:
    def __init__(self, place, bufs, sems, out_ref):
        self.place = place
        self.part, self.ra, self.sb, self.rb, self.sc, self.rc, self.rd = bufs
        self.a_s, self.a_r, self.b_s, self.b_r, self.c_s, self.c_r, self.d_s, self.d_r = sems
        self.out_ref = out_ref
        self.sends = []
        self.split = self.rd.shape[1] != self.out_ref.shape[0]

    def send(self, src, dst, send_sem, recv_sem, where):
        copy = pltpu.make_async_remote_copy(
            src_ref=src, dst_ref=dst, send_sem=send_sem, recv_sem=recv_sem,
            device_id=where, device_id_type=MESH,
        )
        copy.start()
        self.sends.append(copy)

    def arrived(self, dst, send_sem, recv_sem, where):
        pltpu.make_async_remote_copy(
            src_ref=dst, dst_ref=dst, send_sem=send_sem, recv_sem=recv_sem,
            device_id=where, device_id_type=MESH,
        ).wait_recv()

    def put(self, value):
        x_count, n = self.part.shape[1], self.part.shape[2]
        for r in range(2 * x_count):
            self.part[r % 2, r // 2] = value[r * n : (r + 1) * n].astype(BF16)

    def stage_a(self):
        core, peer = self.place["core"], self.place["peer"]
        self.send(self.part.at[1 - core], self.ra, self.a_s, self.a_r, {"dp": peer})

    def stage_b(self):
        core, peer, x, xs = (self.place[k] for k in ("core", "peer", "x", "x_count"))
        self.arrived(self.ra, self.a_s, self.a_r, {"dp": peer})
        for i in range(xs):
            self.sb[i] = (self.part.at[core, i][...].astype(F32) + self.ra[i].astype(F32)).astype(BF16)
        for j in range(1, xs):
            to = lax.rem(x + j, xs)
            self.send(self.sb.at[to], self.rb.at[x], self.b_s.at[j], self.b_r.at[x], {"dp": 2 * to + core})

    def stage_c(self):
        core, x, xs, z, zs = (self.place[k] for k in ("core", "x", "x_count", "z", "z_count"))
        total = self.sb.at[x][...].astype(F32)
        for j in range(1, xs):
            frm = lax.rem(x + xs - j, xs)
            self.arrived(self.rb.at[frm], self.b_s.at[j], self.b_r.at[frm], {"dp": 2 * frm + core})
            total = total + self.rb.at[frm][...].astype(F32)
        if self.split:
            self.sc[...] = total.astype(BF16).reshape(self.sc.shape)
            for j in range(1, zs):
                to = lax.rem(z + j, zs)
                self.send(self.sc.at[to], self.rc.at[z], self.c_s.at[j], self.c_r.at[z], {"graph": to})
        else:
            self.rd.at[z][...] = total.astype(BF16)
            self.spread()

    def spread(self):
        z, zs = self.place["z"], self.place["z_count"]
        for j in range(1, zs):
            to = lax.rem(z + j, zs)
            self.send(self.rd.at[z], self.rd.at[z], self.d_s.at[j], self.d_r.at[z], {"graph": to})

    def stage_d(self):
        z, zs = self.place["z"], self.place["z_count"]
        if self.split:
            total = self.sc.at[z][...].astype(F32)
            for j in range(1, zs):
                frm = lax.rem(z + zs - j, zs)
                self.arrived(self.rc.at[frm], self.c_s.at[j], self.c_r.at[frm], {"graph": frm})
                total = total + self.rc.at[frm][...].astype(F32)
            self.rd.at[z][...] = total.astype(BF16)
            self.spread()

    def finish(self):
        z, zs = self.place["z"], self.place["z_count"]
        for j in range(1, zs):
            frm = lax.rem(z + zs - j, zs)
            self.arrived(self.rd.at[frm], self.d_s.at[j], self.d_r.at[frm], {"graph": frm})
        if self.split:
            self.out_ref[...] = self.rd[...].astype(F32).reshape(self.out_ref.shape)
        else:
            total = self.rd[0].astype(F32)
            for i in range(1, zs):
                total = total + self.rd[i].astype(F32)
            self.out_ref[...] = total


def kernel(
    x_count, z_count,
    feat_ref, cot_hbm, frac_hbm, lattice_hbm, count_hbm, target_hbm, source_hbm, shift_hbm,
    win_ref, wout_ref, wrad_ref,
    new_hbm, gf_hbm, gin_hbm, gout_hbm, grad_hbm,
    new_ref, gf_ref, gin_ref, gout_ref, grad_ref, full_in, full_out, full_rad, feat_pad, frac_pad, proj, rows_e, msg_e, dmsg_e, gates, dgates,
    table, columns, basis_l, basis_r, pre, summed_s, dpre_s, dsum_s, d_pad, rim_lo, rim_hi, dproj_s,
    cot_ref, frac_ref, frac_l, frac_r, lattice_ref, count_ref, target_ref, source_ref, shift_ref,
    w_send, w_recv, h_send, h_recv, load_sem, store_sem, *red_scratch,
):
    comps, atoms, channels = feat_ref.shape
    edges = target_ref.shape[1]
    padded = atoms + 2 * RIM
    z = lax.axis_index("graph")
    d = lax.axis_index("dp")
    x, core = lax.div(d, 2), lax.rem(d, 2)
    peer = 2 * x + 1 - core
    place = dict(core=core, peer=peer, x=x, x_count=x_count, z=z, z_count=z_count)
    sends = []
    loads = [
        pltpu.make_async_copy(src, dst, load_sem.at[i])
        for i, (src, dst) in enumerate(
            (
                (feat_ref, feat_pad.at[:, RIM : RIM + atoms]),
                (win_ref, full_in.at[d]),
                (wout_ref, full_out.at[d]),
                (cot_hbm, cot_ref),
                (frac_hbm, frac_ref),
                (lattice_hbm, lattice_ref),
                (count_hbm, count_ref),
                (target_hbm, target_ref),
                (source_hbm, source_ref),
                (shift_hbm, shift_ref),
            )
        )
    ]
    rad_count, rad_wide = wrad_ref.shape
    pieces = rad_wide // full_rad.shape[2]
    rad_loads = [
        pltpu.make_async_copy(
            wrad_ref.at[:, i * rad_wide // pieces : (i + 1) * rad_wide // pieces],
            full_rad.at[d, i * rad_count : (i + 1) * rad_count],
            load_sem.at[10 + i],
        )
        for i in range(pieces)
    ]
    for load in loads[4:] + rad_loads + loads[:4]:
        load.start()

    barrier = pltpu.get_barrier_semaphore()
    for j in range(1, z_count):
        pl.semaphore_signal(barrier, inc=1, device_id={"graph": lax.rem(z + j, z_count)}, device_id_type=MESH)
    for j in range(1, x_count):
        pl.semaphore_signal(
            barrier, inc=1, device_id={"dp": 2 * lax.rem(x + j, x_count) + core}, device_id_type=MESH
        )
    pl.semaphore_signal(barrier, inc=1, device_id={"dp": peer}, device_id_type=MESH)
    pl.semaphore_wait(barrier, z_count - 1 + x_count)

    def remote(src, dst, send_sem, recv_sem, where):
        return pltpu.make_async_remote_copy(
            src_ref=src, dst_ref=dst, send_sem=send_sem, recv_sem=recv_sem,
            device_id=where, device_id_type=MESH,
        )

    def send(*args):
        copy = remote(*args)
        copy.start()
        sends.append(copy)

    def gather_start(i, w_ref, full):
        for j in range(1, x_count):
            to = 2 * lax.rem(x + j, x_count) + core
            send(w_ref, full.at[d], w_send.at[i, j], w_recv.at[i, d], {"dp": to})
        send(w_ref, full.at[d], w_send.at[i, 0], w_recv.at[i, d], {"dp": peer})

    def gather_forward(i, full):
        for j in range(1, x_count):
            frm = 2 * lax.rem(x + x_count - j, x_count) + core
            remote(full.at[frm], full.at[frm], w_send.at[i, j], w_recv.at[i, frm], {"dp": frm}).wait_recv()
            send(full.at[frm], full.at[frm], w_send.at[i, x_count + j - 1], w_recv.at[i, frm], {"dp": peer})

    def gather_finish(i, full):
        for j in range(x_count):
            frm = 2 * lax.rem(x + x_count - j, x_count) + 1 - core
            remote(full.at[frm], full.at[frm], w_send.at[i, 0], w_recv.at[i, frm], {"dp": peer}).wait_recv()

    right = {"graph": lax.rem(z + 1, z_count)}
    left = {"graph": lax.rem(z + z_count - 1, z_count)}
    last = atoms - RIM
    ahead = RIM + atoms
    send(frac_hbm, frac_l, h_send.at[0], h_recv.at[0], right)
    send(frac_hbm, frac_r, h_send.at[1], h_recv.at[1], left)
    gather_start(0, win_ref, full_in)
    send(feat_ref.at[:, last:atoms], feat_pad.at[:, 0:RIM], h_send.at[2], h_recv.at[2], right)
    send(feat_ref.at[:, 0:RIM], feat_pad.at[:, ahead:padded], h_send.at[3], h_recv.at[3], left)
    for load in rad_loads:
        load.wait()
    gather_start(1, full_rad.at[d], full_rad)

    for load in loads[4:]:
        load.wait()
    remote(frac_l, frac_l, h_send.at[0], h_recv.at[0], left).wait_recv()
    remote(frac_r, frac_r, h_send.at[1], h_recv.at[1], right).wait_recv()
    table[...] = jnp.zeros_like(table)
    for i in range(3):
        table[i : i + 1, 0:RIM] = frac_l[i, :, last:atoms]
        table[i : i + 1, RIM:ahead] = frac_ref[i]
        table[i : i + 1, ahead:padded] = frac_r[i, :, 0:RIM]
    frac_pad[...] = table[:, 0:128].T

    tgt_row = target_ref[...].astype(F32)
    total_atoms = z_count * atoms
    local = source_ref[...] - z * atoms + RIM
    local = jnp.where(local < 0, local + total_atoms, local)
    local = jnp.where(local >= total_atoms, local - total_atoms, local)
    src_row = local.astype(F32)
    live = lax.broadcasted_iota(jnp.int32, (1, edges), 1) < count_ref[...]
    live = jnp.where(live, 1.0, 0.0)
    hot_src_t = lax.broadcasted_iota(jnp.int32, (padded, edges), 0).astype(F32) == src_row
    hot_tgt_t = lax.broadcasted_iota(jnp.int32, (atoms, edges), 0).astype(F32) == tgt_row
    diffs = []
    for i in range(3):
        f_src = jnp.sum(jnp.where(hot_src_t, frac_pad[0:padded, i : i + 1], 0.0), axis=0, keepdims=True)
        f_tgt = jnp.sum(jnp.where(hot_tgt_t, frac_pad[RIM:ahead, i : i + 1], 0.0), axis=0, keepdims=True)
        diffs.append(f_src + shift_ref[i].astype(F32) - f_tgt)
    displace = [
        sum(diffs[i] * lattice_ref[i, :, j : j + 1] for i in range(3)) for j in range(3)
    ]
    distance = jnp.sqrt(
        displace[0] * displace[0] + displace[1] * displace[1] + displace[2] * displace[2] + 1.0
    )
    ux, uy, uz = (displace[j] / distance for j in range(3))
    envelope = 0.5 * (jnp.cos(math.pi * distance / CUTOFF) + 1.0) * live
    entries = [
        envelope,
        ROOT_THREE * uy,
        ROOT_THREE * uz,
        ROOT_THREE * ux,
        ROOT_FIFTEEN * ux * uy,
        ROOT_FIFTEEN * uy * uz,
        0.5 * ROOT_FIVE * (2.0 * uz * uz - ux * ux - uy * uy),
        ROOT_FIFTEEN * ux * uz,
        0.5 * ROOT_FIFTEEN * (ux * ux - uy * uy),
        distance,
        tgt_row,
        src_row,
    ]
    for i, entry in enumerate(entries):
        table[i : i + 1, :] = entry
    columns[...] = table[...].T
    hot_src = (
        lax.broadcasted_iota(jnp.int32, (edges, padded), 1).astype(F32) == columns[:, 11:12]
    ).astype(BF16)
    hot_tgt = (
        lax.broadcasted_iota(jnp.int32, (edges, atoms), 1).astype(F32) == columns[:, 10:11]
    ).astype(BF16)
    hot_src_t = hot_src_t.astype(BF16)
    hot_tgt_t = hot_tgt_t.astype(BF16)

    ranks, rad_rows, rad_cols = full_rad.shape
    quarter = rad_rows // 2
    slot = lax.broadcasted_iota(jnp.int32, (1, 2 * RB), 1)
    half = (slot >> log2(quarter)) & 1
    index = ((slot >> log2(rad_rows)) << log2(quarter)) + (slot & (quarter - 1))
    centres = CUTOFF * index.astype(F32) / (RB - 1)
    offset = (columns[:, 9:10] - centres) / (2.0 * CUTOFF / RB)
    basis = jnp.exp(-(offset * offset)) * columns[:, 0:1]
    basis_l[...] = jnp.where(half == 0, basis, 0.0).astype(BF16)
    basis_r[...] = jnp.where(half == 1, basis, 0.0).astype(BF16)

    for load in loads[:2]:
        load.wait()
    gather_forward(0, full_in)
    gather_start(2, wout_ref, full_out)
    gather_forward(1, full_rad)
    gather_finish(1, full_rad)
    rad = full_rad[...].reshape(ranks * rad_rows, rad_cols)
    gates[:, :rad_cols] = dot(basis_l[...], rad)
    gates[:, rad_cols:] = dot(basis_r[...], rad)
    gather_finish(0, full_in)
    remote(feat_pad.at[:, 0:RIM], feat_pad.at[:, 0:RIM], h_send.at[2], h_recv.at[2], left).wait_recv()
    remote(feat_pad.at[:, ahead:padded], feat_pad.at[:, ahead:padded], h_send.at[3], h_recv.at[3], right).wait_recv()
    proj[...] = (
        dot(feat_pad[...].reshape(comps * padded, channels), full_in[...].reshape(channels, channels))
        .astype(BF16)
        .reshape(comps, padded, channels)
    )
    for k in range(comps):
        rows_e[k] = dot(hot_src, proj[k]).astype(BF16)
    for load in loads[2:4]:
        load.wait()
    gather_forward(2, full_out)

    def gate_of(rows):
        return [gates[rows, i * channels : (i + 1) * channels] for i in range(3)]

    @pl.loop(0, edges // EDGE_ROWS)
    def _(step):
        rows = pl.ds(pl.multiple_of(step * EDGE_ROWS, EDGE_ROWS), EDGE_ROWS)
        harm = columns[rows, :]
        g0, g1, g2 = gate_of(rows)
        scalars = rows_e[0, rows, :].astype(F32)
        msg_e[0, rows, :] = (g0 * scalars).astype(BF16)
        for k in range(1, comps):
            inner = harm[:, k : k + 1] * scalars + rows_e[k, rows, :].astype(F32)
            msg_e[k, rows, :] = ((g1 if k < 4 else g2) * inner).astype(BF16)

    for k in range(comps):
        summed_s[k] = (0.25 * dot(hot_tgt_t, msg_e[k])).astype(BF16)
    gather_finish(2, full_out)
    w_out = full_out[...].reshape(channels, channels)
    flat = (comps * atoms, channels)
    pre[...] = dot(summed_s[...].reshape(flat), w_out).reshape(comps, atoms, channels)

    @pl.loop(0, atoms // 16)
    def _(step):
        rows = pl.ds(pl.multiple_of(step * 16, 16), 16)
        shifted = pl.ds(pl.multiple_of(step * 16 + RIM, 16), 16)
        p0 = pre[0, rows, :]
        gate = jax.nn.sigmoid(p0)
        total = jnp.zeros_like(gate)
        for k in range(comps):
            p = pre[k, rows, :]
            u = cot_ref[k, rows, :].astype(F32)
            total = total + u * p
            new_ref[k, rows, :] = (feat_pad[k, shifted, :].astype(F32) + p * gate).astype(BF16)
            if k:
                dpre_s[k, rows, :] = (u * gate).astype(BF16)
        u0 = cot_ref[0, rows, :].astype(F32)
        dpre_s[0, rows, :] = (u0 * gate + gate * (1.0 - gate) * total).astype(BF16)

    stores = []

    def store(i, src, dst):
        copy = pltpu.make_async_copy(src, dst, store_sem.at[i])
        copy.start()
        stores.append(copy)

    store(0, new_ref, new_hbm)
    scale = 1.0 / (z_count * atoms)
    count = len(red_scratch) // 3
    reds = [
        Reduction(place, red_scratch[i * count : i * count + 7], red_scratch[i * count + 7 : (i + 1) * count], out)
        for i, out in enumerate((gout_ref, grad_ref, gin_ref))
    ]
    red_out, red_rad, red_in = reds
    across = ((0,), (0,))
    red_out.put(scale * dot(summed_s[...].reshape(flat), dpre_s[...].reshape(flat), across))
    red_out.stage_a()
    dsum_s[...] = (
        (0.25 * dot(dpre_s[...].reshape(flat), w_out, ((1,), (1,)))).astype(BF16).reshape(comps, atoms, channels)
    )
    red_out.stage_b()
    for k in range(comps):
        dmsg_e[k] = dot(hot_tgt, dsum_s[k]).astype(BF16)

    @pl.loop(0, edges // EDGE_ROWS)
    def _(step):
        rows = pl.ds(pl.multiple_of(step * EDGE_ROWS, EDGE_ROWS), EDGE_ROWS)
        harm = columns[rows, :]
        g0, g1, g2 = gate_of(rows)
        scalars = rows_e[0, rows, :].astype(F32)
        d0 = dmsg_e[0, rows, :].astype(F32)
        dgates[rows, 0:channels] = (d0 * scalars).astype(BF16)
        d_scalars = d0 * g0
        for lo, hi, gate in ((1, 4, g1), (4, 9, g2)):
            mixed = jnp.zeros_like(d0)
            plain = jnp.zeros_like(d0)
            for k in range(lo, hi):
                dk = dmsg_e[k, rows, :].astype(F32)
                mixed = mixed + dk * harm[:, k : k + 1]
                plain = plain + dk * rows_e[k, rows, :].astype(F32)
                msg_e[k, rows, :] = (gate * dk).astype(BF16)
            block = 1 if lo == 1 else 2
            dgates[rows, block * channels : (block + 1) * channels] = (mixed * scalars + plain).astype(BF16)
            d_scalars = d_scalars + gate * mixed
        msg_e[0, rows, :] = d_scalars.astype(BF16)

    red_rad.put(
        scale
        * (
            dot(basis_l[...], dgates[:, :rad_cols], across)
            + dot(basis_r[...], dgates[:, rad_cols:], across)
        )
    )
    red_rad.stage_a()
    red_out.stage_c()
    for k in range(comps):
        d_pad[k] = dot(hot_src_t, msg_e[k]).astype(BF16)
    send(d_pad.at[:, 0:RIM], rim_hi, h_send.at[4], h_recv.at[4], left)
    send(d_pad.at[:, ahead:padded], rim_lo, h_send.at[5], h_recv.at[5], right)
    red_rad.stage_b()
    red_in.put(
        scale
        * dot(
            feat_pad[...].reshape(comps * padded, channels),
            d_pad[...].reshape(comps * padded, channels),
            across,
        )
    )
    red_in.stage_a()
    red_out.stage_d()
    red_in.stage_b()
    red_rad.stage_c()
    red_in.stage_c()
    red_rad.stage_d()
    remote(rim_hi, rim_hi, h_send.at[4], h_recv.at[4], right).wait_recv()
    remote(rim_lo, rim_lo, h_send.at[5], h_recv.at[5], left).wait_recv()
    dproj_s[...] = d_pad[:, RIM:ahead, :]
    dproj_s[:, 0:RIM, :] = (dproj_s[:, 0:RIM, :].astype(F32) + rim_lo[...].astype(F32)).astype(BF16)
    dproj_s[:, last:atoms, :] = (dproj_s[:, last:atoms, :].astype(F32) + rim_hi[...].astype(F32)).astype(BF16)
    back = dot(dproj_s[...].reshape(flat), full_in[...].reshape(channels, channels), ((1,), (1,)))
    gf_ref[...] = (
        (cot_ref[...].reshape(flat).astype(F32) + back).astype(BF16).reshape(comps, atoms, channels)
    )
    store(1, gf_ref, gf_hbm)
    red_in.stage_d()
    red_out.finish()
    store(2, gout_ref, gout_hbm)
    red_rad.finish()
    for i in range(2):
        store(
            3 + i,
            grad_ref.at[i * quarter : (i + 1) * quarter],
            grad_hbm.at[:, i * rad_cols : (i + 1) * rad_cols],
        )
    red_in.finish()
    store(5, gin_ref, gin_hbm)
    for copy in stores:
        copy.wait()
    for red in reds:
        for copy in red.sends:
            copy.wait_send()
    for copy in sends:
        copy.wait_send()


def hand_over(*refs):
    sem = refs[-1]
    copies = [pltpu.make_async_copy(refs[i], refs[5 + i], sem.at[i]) for i in range(5)]
    for copy in copies:
        copy.start()
    for copy in copies:
        copy.wait()


def body(x_count, z_count, node_feats, frac_pos, lattice, edge_count, edge_target, edge_source,
         edge_shift, cotangent, w_in, w_out, w_rad):
    atoms, comps, channels = node_feats.shape[1:]
    edges = edge_target.shape[1]
    padded = atoms + 2 * RIM
    dp = 2 * x_count
    across = lambda array: jnp.transpose(array, (1, 0, 2))
    feats = jnp.transpose(node_feats[0], (1, 0, 2))
    cot = jnp.transpose(cotangent[0], (1, 0, 2))
    rad_cols = w_rad.shape[1] // 2
    rows, rad_rows = w_in.shape[0], 2 * w_rad.shape[0]
    rad = w_rad
    if w_rad.shape[0] % 16:
        rad = jnp.concatenate([w_rad[:, :rad_cols], w_rad[:, rad_cols:]], axis=0)

    vmem = lambda shape, dtype=BF16: pltpu.VMEM(shape, dtype)
    dma = pltpu.SemaphoreType.DMA
    scratch = [
        vmem((comps, atoms, channels)), vmem((comps, atoms, channels)), vmem((rows, channels), F32),
        vmem((rows, channels), F32), vmem((rad_rows, rad_cols), F32),
        vmem((dp, rows, channels)), vmem((dp, rows, channels)), vmem((dp, rad_rows, rad_cols)),
        vmem((comps, padded, channels)), vmem((128, 128), F32), vmem((comps, padded, channels)),
        vmem((comps, edges, channels)), vmem((comps, edges, channels)), vmem((comps, edges, channels)),
        vmem((edges, 3 * channels), F32), vmem((edges, 3 * channels)),
        vmem((128, edges), F32), vmem((edges, 128), F32), vmem((edges, 2 * RB)), vmem((edges, 2 * RB)),
        vmem((comps, atoms, channels), F32), vmem((comps, atoms, channels)),
        vmem((comps, atoms, channels)), vmem((comps, atoms, channels)),
        vmem((comps, padded, channels)), vmem((comps, RIM, channels)), vmem((comps, RIM, channels)),
        vmem((comps, atoms, channels)),
        vmem((comps, atoms, channels)), vmem((3, 1, atoms), F32), vmem((3, 1, atoms), F32), vmem((3, 1, atoms), F32),
        vmem((3, 1, 3), F32), vmem((1, 1), jnp.int32), vmem((1, edges), jnp.int32),
        vmem((1, edges), jnp.int32), vmem((3, 1, edges), jnp.int32),
        dma((3, 2 * x_count)), dma((3, dp)), dma((6,)), dma((6,)), dma((12,)), dma((6,)),
    ]
    for n, cols in ((rows, channels), (rad_rows, rad_cols), (rows, channels)):
        piece = n // z_count if n % (16 * z_count) == 0 else n
        scratch += [
            vmem((2, x_count, n, cols)), vmem((x_count, n, cols)), vmem((x_count, n, cols)),
            vmem((x_count, n, cols)), vmem((n // piece, piece, cols)), vmem((z_count, piece, cols)),
            vmem((z_count, piece, cols)),
            dma, dma, dma((x_count,)), dma((x_count,)), dma((z_count,)), dma((z_count,)),
            dma((z_count,)), dma((z_count,)),
        ]
    outs = [
        jax.ShapeDtypeStruct((comps, atoms, channels), BF16),
        jax.ShapeDtypeStruct((comps, atoms, channels), BF16),
        jax.ShapeDtypeStruct((rows, channels), F32),
        jax.ShapeDtypeStruct((rows, channels), F32),
        jax.ShapeDtypeStruct((rad_rows // 2, 2 * rad_cols), F32),
    ]
    results = pl.pallas_call(
        functools.partial(kernel, x_count, z_count),
        out_shape=outs,
        in_specs=[pl.BlockSpec(memory_space=pltpu.HBM)] * 11,
        out_specs=[pl.BlockSpec(memory_space=pltpu.HBM)] * 5,
        scratch_shapes=scratch,
        compiler_params=pltpu.CompilerParams(
            collective_id=0, has_side_effects=True, vmem_limit_bytes=64 * 1024 * 1024
        ),
    )(
        feats, cot, across(frac_pos), across(lattice), edge_count, edge_target, edge_source, across(edge_shift),
        w_in, w_out, rad,
    )
    new, grad_feats, g_in, g_out, g_rad = pl.pallas_call(
        hand_over,
        out_shape=outs,
        in_specs=[pl.BlockSpec(memory_space=pltpu.HBM)] * 5,
        out_specs=[pl.BlockSpec(memory_space=pltpu.HBM)] * 5,
        scratch_shapes=[dma((5,))],
        compiler_params=pltpu.CompilerParams(vmem_limit_bytes=64 * 1024 * 1024),
    )(*results)
    return (across(new)[None], across(grad_feats)[None], g_in, g_out, g_rad)


def solution(mesh):
    return jax.shard_map(
        functools.partial(body, mesh.shape["dp"] // 2, mesh.shape["graph"]),
        mesh=mesh,
        in_specs=(
            P(("groups", "dp"), "graph", None, None),
            P(("groups", "dp"), None, "graph"),
            P(("groups", "dp"), None, None),
            P(("groups", "dp"), "graph"),
            P(("groups", "dp"), "graph"),
            P(("groups", "dp"), "graph"),
            P(("groups", "dp"), None, "graph"),
            P(("groups", "dp"), "graph", None, None),
            P("dp", None),
            P("dp", None),
            P("dp", None),
        ),
        out_specs=(
            P(("groups", "dp"), "graph", None, None),
            P(("groups", "dp"), "graph", None, None),
            P(("groups", "dp"), None),
            P(("groups", "dp"), None),
            P(("groups", "dp"), None),
        ),
        check_vma=False,
    )
```

```python
import functools
import math

import jax
import jax.numpy as jnp
from jax import lax
from jax.experimental import pallas as pl
from jax.experimental.pallas import tpu as pltpu
from jax.sharding import PartitionSpec as P

RB = 128
RIM = 16
EDGE_ROWS = 16
CUTOFF = 48.0
ROOT_THREE = math.sqrt(3.0)
ROOT_FIVE = math.sqrt(5.0)
ROOT_FIFTEEN = math.sqrt(15.0)
MESH = pl.DeviceIdType.MESH
F32 = jnp.float32
BF16 = jnp.bfloat16


def dot(a, b, dims=((1,), (0,))):
    return lax.dot_general(a, b, (dims, ((), ())), preferred_element_type=F32)


def log2(value):
    bits = value.bit_length() - 1
    assert 1 << bits == value
    return bits


class Reduction:
    def __init__(self, place, bufs, sems, out_ref):
        self.place = place
        self.part, self.ra, self.sb, self.rb, self.sc, self.rc, self.rd = bufs
        self.a_s, self.a_r, self.b_s, self.b_r, self.c_s, self.c_r, self.d_s, self.d_r = sems
        self.out_ref = out_ref
        self.sends = []
        self.split = self.rd.shape[1] != self.out_ref.shape[0]

    def send(self, src, dst, send_sem, recv_sem, where):
        copy = pltpu.make_async_remote_copy(
            src_ref=src, dst_ref=dst, send_sem=send_sem, recv_sem=recv_sem,
            device_id=where, device_id_type=MESH,
        )
        copy.start()
        self.sends.append(copy)

    def arrived(self, dst, send_sem, recv_sem, where):
        pltpu.make_async_remote_copy(
            src_ref=dst, dst_ref=dst, send_sem=send_sem, recv_sem=recv_sem,
            device_id=where, device_id_type=MESH,
        ).wait_recv()

    def put(self, value):
        x_count, n = self.part.shape[1], self.part.shape[2]
        for r in range(2 * x_count):
            self.part[r % 2, r // 2] = value[r * n : (r + 1) * n].astype(BF16)

    def stage_a(self):
        core, peer = self.place["core"], self.place["peer"]
        self.send(self.part.at[1 - core], self.ra, self.a_s, self.a_r, {"dp": peer})

    def stage_b(self):
        core, peer, x, xs = (self.place[k] for k in ("core", "peer", "x", "x_count"))
        self.arrived(self.ra, self.a_s, self.a_r, {"dp": peer})
        for i in range(xs):
            self.sb[i] = (self.part.at[core, i][...].astype(F32) + self.ra[i].astype(F32)).astype(BF16)
        for j in range(1, xs):
            to = lax.rem(x + j, xs)
            self.send(self.sb.at[to], self.rb.at[x], self.b_s.at[j], self.b_r.at[x], {"dp": 2 * to + core})

    def stage_c(self):
        core, x, xs, z, zs = (self.place[k] for k in ("core", "x", "x_count", "z", "z_count"))
        total = self.sb.at[x][...].astype(F32)
        for j in range(1, xs):
            frm = lax.rem(x + xs - j, xs)
            self.arrived(self.rb.at[frm], self.b_s.at[j], self.b_r.at[frm], {"dp": 2 * frm + core})
            total = total + self.rb.at[frm][...].astype(F32)
        if self.split:
            self.sc[...] = total.astype(BF16).reshape(self.sc.shape)
            for j in range(1, zs):
                to = lax.rem(z + j, zs)
                self.send(self.sc.at[to], self.rc.at[z], self.c_s.at[j], self.c_r.at[z], {"graph": to})
        else:
            self.rd.at[z][...] = total.astype(BF16)
            self.spread()

    def spread(self):
        z, zs = self.place["z"], self.place["z_count"]
        for j in range(1, zs):
            to = lax.rem(z + j, zs)
            self.send(self.rd.at[z], self.rd.at[z], self.d_s.at[j], self.d_r.at[z], {"graph": to})

    def stage_d(self):
        z, zs = self.place["z"], self.place["z_count"]
        if self.split:
            total = self.sc.at[z][...].astype(F32)
            for j in range(1, zs):
                frm = lax.rem(z + zs - j, zs)
                self.arrived(self.rc.at[frm], self.c_s.at[j], self.c_r.at[frm], {"graph": frm})
                total = total + self.rc.at[frm][...].astype(F32)
            self.rd.at[z][...] = total.astype(BF16)
            self.spread()

    def finish(self):
        z, zs = self.place["z"], self.place["z_count"]
        for j in range(1, zs):
            frm = lax.rem(z + zs - j, zs)
            self.arrived(self.rd.at[frm], self.d_s.at[j], self.d_r.at[frm], {"graph": frm})
        if self.split:
            self.out_ref[...] = self.rd[...].astype(F32).reshape(self.out_ref.shape)
        else:
            total = self.rd[0].astype(F32)
            for i in range(1, zs):
                total = total + self.rd[i].astype(F32)
            self.out_ref[...] = total


def kernel(
    x_count, z_count,
    feat_ref, cot_hbm, frac_hbm, lattice_hbm, count_hbm, target_hbm, source_hbm, shift_hbm,
    win_ref, wout_ref, wrad_ref,
    new_hbm, gf_hbm, gin_hbm, gout_hbm, grad_hbm,
    new_ref, gf_ref, gin_ref, gout_ref, grad_ref, full_in, full_out, full_rad, feat_pad, frac_pad, proj, rows_e, msg_e, dmsg_e, gates, dgates,
    table, columns, basis_l, basis_r, pre, summed_s, dpre_s, dsum_s, d_pad, rim_lo, rim_hi, dproj_s,
    cot_ref, frac_ref, frac_l, frac_r, lattice_ref, count_ref, target_ref, source_ref, shift_ref,
    w_send, w_recv, h_send, h_recv, load_sem, store_sem, *red_scratch,
):
    comps, atoms, channels = feat_ref.shape
    edges = target_ref.shape[1]
    padded = atoms + 2 * RIM
    z = lax.axis_index("graph")
    d = lax.axis_index("dp")
    x, core = lax.div(d, 2), lax.rem(d, 2)
    peer = 2 * x + 1 - core
    place = dict(core=core, peer=peer, x=x, x_count=x_count, z=z, z_count=z_count)
    sends = []
    loads = [
        pltpu.make_async_copy(src, dst, load_sem.at[i])
        for i, (src, dst) in enumerate(
            (
                (feat_ref, feat_pad.at[:, RIM : RIM + atoms]),
                (win_ref, full_in.at[d]),
                (wout_ref, full_out.at[d]),
                (cot_hbm, cot_ref),
                (frac_hbm, frac_ref),
                (lattice_hbm, lattice_ref),
                (count_hbm, count_ref),
                (target_hbm, target_ref),
                (source_hbm, source_ref),
                (shift_hbm, shift_ref),
            )
        )
    ]
    rad_count, rad_wide = wrad_ref.shape
    pieces = rad_wide // full_rad.shape[2]
    rad_loads = [
        pltpu.make_async_copy(
            wrad_ref.at[:, i * rad_wide // pieces : (i + 1) * rad_wide // pieces],
            full_rad.at[d, i * rad_count : (i + 1) * rad_count],
            load_sem.at[10 + i],
        )
        for i in range(pieces)
    ]
    for load in loads[4:] + rad_loads + loads[:4]:
        load.start()

    barrier = pltpu.get_barrier_semaphore()
    for j in range(1, z_count):
        pl.semaphore_signal(barrier, inc=1, device_id={"graph": lax.rem(z + j, z_count)}, device_id_type=MESH)
    for j in range(1, x_count):
        pl.semaphore_signal(
            barrier, inc=1, device_id={"dp": 2 * lax.rem(x + j, x_count) + core}, device_id_type=MESH
        )
    pl.semaphore_signal(barrier, inc=1, device_id={"dp": peer}, device_id_type=MESH)
    pl.semaphore_wait(barrier, z_count - 1 + x_count)

    def remote(src, dst, send_sem, recv_sem, where):
        return pltpu.make_async_remote_copy(
            src_ref=src, dst_ref=dst, send_sem=send_sem, recv_sem=recv_sem,
            device_id=where, device_id_type=MESH,
        )

    def send(*args):
        copy = remote(*args)
        copy.start()
        sends.append(copy)

    def gather_start(i, w_ref, full):
        for j in range(1, x_count):
            to = 2 * lax.rem(x + j, x_count) + core
            send(w_ref, full.at[d], w_send.at[i, j], w_recv.at[i, d], {"dp": to})
        send(w_ref, full.at[d], w_send.at[i, 0], w_recv.at[i, d], {"dp": peer})

    def gather_forward(i, full):
        for j in range(1, x_count):
            frm = 2 * lax.rem(x + x_count - j, x_count) + core
            remote(full.at[frm], full.at[frm], w_send.at[i, j], w_recv.at[i, frm], {"dp": frm}).wait_recv()
            send(full.at[frm], full.at[frm], w_send.at[i, x_count + j - 1], w_recv.at[i, frm], {"dp": peer})

    def gather_finish(i, full):
        for j in range(x_count):
            frm = 2 * lax.rem(x + x_count - j, x_count) + 1 - core
            remote(full.at[frm], full.at[frm], w_send.at[i, 0], w_recv.at[i, frm], {"dp": peer}).wait_recv()

    right = {"graph": lax.rem(z + 1, z_count)}
    left = {"graph": lax.rem(z + z_count - 1, z_count)}
    last = atoms - RIM
    ahead = RIM + atoms
    send(frac_hbm, frac_l, h_send.at[0], h_recv.at[0], right)
    send(frac_hbm, frac_r, h_send.at[1], h_recv.at[1], left)
    gather_start(0, win_ref, full_in)
    send(feat_ref.at[:, last:atoms], feat_pad.at[:, 0:RIM], h_send.at[2], h_recv.at[2], right)
    send(feat_ref.at[:, 0:RIM], feat_pad.at[:, ahead:padded], h_send.at[3], h_recv.at[3], left)
    for load in rad_loads:
        load.wait()
    gather_start(1, full_rad.at[d], full_rad)

    for load in loads[4:]:
        load.wait()
    remote(frac_l, frac_l, h_send.at[0], h_recv.at[0], left).wait_recv()
    remote(frac_r, frac_r, h_send.at[1], h_recv.at[1], right).wait_recv()
    table[...] = jnp.zeros_like(table)
    for i in range(3):
        table[i : i + 1, 0:RIM] = frac_l[i, :, last:atoms]
        table[i : i + 1, RIM:ahead] = frac_ref[i]
        table[i : i + 1, ahead:padded] = frac_r[i, :, 0:RIM]
    frac_pad[...] = table[:, 0:128].T

    tgt_row = target_ref[...].astype(F32)
    total_atoms = z_count * atoms
    local = source_ref[...] - z * atoms + RIM
    local = jnp.where(local < 0, local + total_atoms, local)
    local = jnp.where(local >= total_atoms, local - total_atoms, local)
    src_row = local.astype(F32)
    live = lax.broadcasted_iota(jnp.int32, (1, edges), 1) < count_ref[...]
    live = jnp.where(live, 1.0, 0.0)
    hot_src_t = lax.broadcasted_iota(jnp.int32, (padded, edges), 0).astype(F32) == src_row
    hot_tgt_t = lax.broadcasted_iota(jnp.int32, (atoms, edges), 0).astype(F32) == tgt_row
    diffs = []
    for i in range(3):
        f_src = jnp.sum(jnp.where(hot_src_t, frac_pad[0:padded, i : i + 1], 0.0), axis=0, keepdims=True)
        f_tgt = jnp.sum(jnp.where(hot_tgt_t, frac_pad[RIM:ahead, i : i + 1], 0.0), axis=0, keepdims=True)
        diffs.append(f_src + shift_ref[i].astype(F32) - f_tgt)
    displace = [
        sum(diffs[i] * lattice_ref[i, :, j : j + 1] for i in range(3)) for j in range(3)
    ]
    distance = jnp.sqrt(
        displace[0] * displace[0] + displace[1] * displace[1] + displace[2] * displace[2] + 1.0
    )
    ux, uy, uz = (displace[j] / distance for j in range(3))
    envelope = 0.5 * (jnp.cos(math.pi * distance / CUTOFF) + 1.0) * live
    entries = [
        envelope,
        ROOT_THREE * uy,
        ROOT_THREE * uz,
        ROOT_THREE * ux,
        ROOT_FIFTEEN * ux * uy,
        ROOT_FIFTEEN * uy * uz,
        0.5 * ROOT_FIVE * (2.0 * uz * uz - ux * ux - uy * uy),
        ROOT_FIFTEEN * ux * uz,
        0.5 * ROOT_FIFTEEN * (ux * ux - uy * uy),
        distance,
        tgt_row,
        src_row,
    ]
    for i, entry in enumerate(entries):
        table[i : i + 1, :] = entry
    columns[...] = table[...].T
    hot_src = (
        lax.broadcasted_iota(jnp.int32, (edges, padded), 1).astype(F32) == columns[:, 11:12]
    ).astype(BF16)
    hot_tgt = (
        lax.broadcasted_iota(jnp.int32, (edges, atoms), 1).astype(F32) == columns[:, 10:11]
    ).astype(BF16)
    hot_src_t = hot_src_t.astype(BF16)
    hot_tgt_t = hot_tgt_t.astype(BF16)

    ranks, rad_rows, rad_cols = full_rad.shape
    quarter = rad_rows // 2
    slot = lax.broadcasted_iota(jnp.int32, (1, 2 * RB), 1)
    half = (slot >> log2(quarter)) & 1
    index = ((slot >> log2(rad_rows)) << log2(quarter)) + (slot & (quarter - 1))
    centres = CUTOFF * index.astype(F32) / (RB - 1)
    offset = (columns[:, 9:10] - centres) / (2.0 * CUTOFF / RB)
    basis = jnp.exp(-(offset * offset)) * columns[:, 0:1]
    basis_l[...] = jnp.where(half == 0, basis, 0.0).astype(BF16)
    basis_r[...] = jnp.where(half == 1, basis, 0.0).astype(BF16)

    for load in loads[:2]:
        load.wait()
    gather_forward(0, full_in)
    gather_start(2, wout_ref, full_out)
    gather_forward(1, full_rad)
    gather_finish(1, full_rad)
    rad = full_rad[...].reshape(ranks * rad_rows, rad_cols)
    gates[:, :rad_cols] = dot(basis_l[...], rad)
    gates[:, rad_cols:] = dot(basis_r[...], rad)
    gather_finish(0, full_in)
    remote(feat_pad.at[:, 0:RIM], feat_pad.at[:, 0:RIM], h_send.at[2], h_recv.at[2], left).wait_recv()
    remote(feat_pad.at[:, ahead:padded], feat_pad.at[:, ahead:padded], h_send.at[3], h_recv.at[3], right).wait_recv()
    proj[...] = (
        dot(feat_pad[...].reshape(comps * padded, channels), full_in[...].reshape(channels, channels))
        .astype(BF16)
        .reshape(comps, padded, channels)
    )
    for k in range(comps):
        rows_e[k] = dot(hot_src, proj[k]).astype(BF16)
    for load in loads[2:4]:
        load.wait()
    gather_forward(2, full_out)

    def gate_of(rows):
        return [gates[rows, i * channels : (i + 1) * channels] for i in range(3)]

    @pl.loop(0, edges // EDGE_ROWS)
    def _(step):
        rows = pl.ds(pl.multiple_of(step * EDGE_ROWS, EDGE_ROWS), EDGE_ROWS)
        harm = columns[rows, :]
        g0, g1, g2 = gate_of(rows)
        scalars = rows_e[0, rows, :].astype(F32)
        msg_e[0, rows, :] = (g0 * scalars).astype(BF16)
        for k in range(1, comps):
            inner = harm[:, k : k + 1] * scalars + rows_e[k, rows, :].astype(F32)
            msg_e[k, rows, :] = ((g1 if k < 4 else g2) * inner).astype(BF16)

    for k in range(comps):
        summed_s[k] = (0.25 * dot(hot_tgt_t, msg_e[k])).astype(BF16)
    gather_finish(2, full_out)
    w_out = full_out[...].reshape(channels, channels)
    flat = (comps * atoms, channels)
    pre[...] = dot(summed_s[...].reshape(flat), w_out).reshape(comps, atoms, channels)

    @pl.loop(0, atoms // 16)
    def _(step):
        rows = pl.ds(pl.multiple_of(step * 16, 16), 16)
        shifted = pl.ds(pl.multiple_of(step * 16 + RIM, 16), 16)
        p0 = pre[0, rows, :]
        gate = jax.nn.sigmoid(p0)
        total = jnp.zeros_like(gate)
        for k in range(comps):
            p = pre[k, rows, :]
            u = cot_ref[k, rows, :].astype(F32)
            total = total + u * p
            new_ref[k, rows, :] = (feat_pad[k, shifted, :].astype(F32) + p * gate).astype(BF16)
            if k:
                dpre_s[k, rows, :] = (u * gate).astype(BF16)
        u0 = cot_ref[0, rows, :].astype(F32)
        dpre_s[0, rows, :] = (u0 * gate + gate * (1.0 - gate) * total).astype(BF16)

    stores = []

    def store(i, src, dst):
        copy = pltpu.make_async_copy(src, dst, store_sem.at[i])
        copy.start()
        stores.append(copy)

    store(0, new_ref, new_hbm)
    scale = 1.0 / (z_count * atoms)
    count = len(red_scratch) // 3
    reds = [
        Reduction(place, red_scratch[i * count : i * count + 7], red_scratch[i * count + 7 : (i + 1) * count], out)
        for i, out in enumerate((gout_ref, grad_ref, gin_ref))
    ]
    red_out, red_rad, red_in = reds
    across = ((0,), (0,))
    red_out.put(scale * dot(summed_s[...].reshape(flat), dpre_s[...].reshape(flat), across))
    red_out.stage_a()
    dsum_s[...] = (
        (0.25 * dot(dpre_s[...].reshape(flat), w_out, ((1,), (1,)))).astype(BF16).reshape(comps, atoms, channels)
    )
    red_out.stage_b()
    for k in range(comps):
        dmsg_e[k] = dot(hot_tgt, dsum_s[k]).astype(BF16)

    @pl.loop(0, edges // EDGE_ROWS)
    def _(step):
        rows = pl.ds(pl.multiple_of(step * EDGE_ROWS, EDGE_ROWS), EDGE_ROWS)
        harm = columns[rows, :]
        g0, g1, g2 = gate_of(rows)
        scalars = rows_e[0, rows, :].astype(F32)
        d0 = dmsg_e[0, rows, :].astype(F32)
        dgates[rows, 0:channels] = (d0 * scalars).astype(BF16)
        d_scalars = d0 * g0
        for lo, hi, gate in ((1, 4, g1), (4, 9, g2)):
            mixed = jnp.zeros_like(d0)
            plain = jnp.zeros_like(d0)
            for k in range(lo, hi):
                dk = dmsg_e[k, rows, :].astype(F32)
                mixed = mixed + dk * harm[:, k : k + 1]
                plain = plain + dk * rows_e[k, rows, :].astype(F32)
                msg_e[k, rows, :] = (gate * dk).astype(BF16)
            block = 1 if lo == 1 else 2
            dgates[rows, block * channels : (block + 1) * channels] = (mixed * scalars + plain).astype(BF16)
            d_scalars = d_scalars + gate * mixed
        msg_e[0, rows, :] = d_scalars.astype(BF16)

    red_rad.put(
        scale
        * (
            dot(basis_l[...], dgates[:, :rad_cols], across)
            + dot(basis_r[...], dgates[:, rad_cols:], across)
        )
    )
    red_rad.stage_a()
    red_out.stage_c()
    for k in range(comps):
        d_pad[k] = dot(hot_src_t, msg_e[k]).astype(BF16)
    send(d_pad.at[:, 0:RIM], rim_hi, h_send.at[4], h_recv.at[4], left)
    send(d_pad.at[:, ahead:padded], rim_lo, h_send.at[5], h_recv.at[5], right)
    red_rad.stage_b()
    red_in.put(
        scale
        * dot(
            feat_pad[...].reshape(comps * padded, channels),
            d_pad[...].reshape(comps * padded, channels),
            across,
        )
    )
    red_in.stage_a()
    red_out.stage_d()
    red_in.stage_b()
    red_rad.stage_c()
    red_in.stage_c()
    red_rad.stage_d()
    remote(rim_hi, rim_hi, h_send.at[4], h_recv.at[4], right).wait_recv()
    remote(rim_lo, rim_lo, h_send.at[5], h_recv.at[5], left).wait_recv()
    dproj_s[...] = d_pad[:, RIM:ahead, :]
    dproj_s[:, 0:RIM, :] = (dproj_s[:, 0:RIM, :].astype(F32) + rim_lo[...].astype(F32)).astype(BF16)
    dproj_s[:, last:atoms, :] = (dproj_s[:, last:atoms, :].astype(F32) + rim_hi[...].astype(F32)).astype(BF16)
    back = dot(dproj_s[...].reshape(flat), full_in[...].reshape(channels, channels), ((1,), (1,)))
    gf_ref[...] = (
        (cot_ref[...].reshape(flat).astype(F32) + back).astype(BF16).reshape(comps, atoms, channels)
    )
    store(1, gf_ref, gf_hbm)
    red_in.stage_d()
    red_out.finish()
    store(2, gout_ref, gout_hbm)
    red_rad.finish()
    for i in range(2):
        store(
            3 + i,
            grad_ref.at[i * quarter : (i + 1) * quarter],
            grad_hbm.at[:, i * rad_cols : (i + 1) * rad_cols],
        )
    red_in.finish()
    store(5, gin_ref, gin_hbm)
    for copy in stores:
        copy.wait()
    for red in reds:
        for copy in red.sends:
            copy.wait_send()
    for copy in sends:
        copy.wait_send()


def hand_over(*refs):
    sources, results, held = refs[:5], refs[5:10], refs[10:15]
    sem = refs[15]
    loads = [pltpu.make_async_copy(sources[i], held[i], sem.at[0, i]) for i in range(5)]
    stores = [pltpu.make_async_copy(held[i], results[i], sem.at[1, i]) for i in range(5)]
    for load in loads:
        load.start()
    for load, store in zip(loads, stores):
        load.wait()
        store.start()
    for store in stores:
        store.wait()


def body(x_count, z_count, node_feats, frac_pos, lattice, edge_count, edge_target, edge_source,
         edge_shift, cotangent, w_in, w_out, w_rad):
    atoms, comps, channels = node_feats.shape[1:]
    edges = edge_target.shape[1]
    padded = atoms + 2 * RIM
    dp = 2 * x_count
    across = lambda array: jnp.transpose(array, (1, 0, 2))
    feats = jnp.transpose(node_feats[0], (1, 0, 2))
    cot = jnp.transpose(cotangent[0], (1, 0, 2))
    rad_cols = w_rad.shape[1] // 2
    rows, rad_rows = w_in.shape[0], 2 * w_rad.shape[0]
    rad = w_rad
    if w_rad.shape[0] % 16:
        rad = jnp.concatenate([w_rad[:, :rad_cols], w_rad[:, rad_cols:]], axis=0)

    vmem = lambda shape, dtype=BF16: pltpu.VMEM(shape, dtype)
    dma = pltpu.SemaphoreType.DMA
    scratch = [
        vmem((comps, atoms, channels)), vmem((comps, atoms, channels)), vmem((rows, channels), F32),
        vmem((rows, channels), F32), vmem((rad_rows, rad_cols), F32),
        vmem((dp, rows, channels)), vmem((dp, rows, channels)), vmem((dp, rad_rows, rad_cols)),
        vmem((comps, padded, channels)), vmem((128, 128), F32), vmem((comps, padded, channels)),
        vmem((comps, edges, channels)), vmem((comps, edges, channels)), vmem((comps, edges, channels)),
        vmem((edges, 3 * channels), F32), vmem((edges, 3 * channels)),
        vmem((128, edges), F32), vmem((edges, 128), F32), vmem((edges, 2 * RB)), vmem((edges, 2 * RB)),
        vmem((comps, atoms, channels), F32), vmem((comps, atoms, channels)),
        vmem((comps, atoms, channels)), vmem((comps, atoms, channels)),
        vmem((comps, padded, channels)), vmem((comps, RIM, channels)), vmem((comps, RIM, channels)),
        vmem((comps, atoms, channels)),
        vmem((comps, atoms, channels)), vmem((3, 1, atoms), F32), vmem((3, 1, atoms), F32), vmem((3, 1, atoms), F32),
        vmem((3, 1, 3), F32), vmem((1, 1), jnp.int32), vmem((1, edges), jnp.int32),
        vmem((1, edges), jnp.int32), vmem((3, 1, edges), jnp.int32),
        dma((3, 2 * x_count)), dma((3, dp)), dma((6,)), dma((6,)), dma((12,)), dma((6,)),
    ]
    for n, cols in ((rows, channels), (rad_rows, rad_cols), (rows, channels)):
        piece = n // z_count if n % (16 * z_count) == 0 else n
        scratch += [
            vmem((2, x_count, n, cols)), vmem((x_count, n, cols)), vmem((x_count, n, cols)),
            vmem((x_count, n, cols)), vmem((n // piece, piece, cols)), vmem((z_count, piece, cols)),
            vmem((z_count, piece, cols)),
            dma, dma, dma((x_count,)), dma((x_count,)), dma((z_count,)), dma((z_count,)),
            dma((z_count,)), dma((z_count,)),
        ]
    outs = [
        jax.ShapeDtypeStruct((comps, atoms, channels), BF16),
        jax.ShapeDtypeStruct((comps, atoms, channels), BF16),
        jax.ShapeDtypeStruct((rows, channels), F32),
        jax.ShapeDtypeStruct((rows, channels), F32),
        jax.ShapeDtypeStruct((rad_rows // 2, 2 * rad_cols), F32),
    ]
    results = pl.pallas_call(
        functools.partial(kernel, x_count, z_count),
        out_shape=outs,
        in_specs=[pl.BlockSpec(memory_space=pltpu.HBM)] * 11,
        out_specs=[pl.BlockSpec(memory_space=pltpu.HBM)] * 5,
        scratch_shapes=scratch,
        compiler_params=pltpu.CompilerParams(
            collective_id=0, has_side_effects=True, vmem_limit_bytes=64 * 1024 * 1024
        ),
    )(
        feats, cot, across(frac_pos), across(lattice), edge_count, edge_target, edge_source, across(edge_shift),
        w_in, w_out, rad,
    )
    new, grad_feats, g_in, g_out, g_rad = pl.pallas_call(
        hand_over,
        out_shape=outs,
        in_specs=[pl.BlockSpec(memory_space=pltpu.HBM)] * 5,
        out_specs=[pl.BlockSpec(memory_space=pltpu.HBM)] * 5,
        scratch_shapes=[vmem(out.shape, out.dtype) for out in outs] + [dma((2, 5))],
        compiler_params=pltpu.CompilerParams(vmem_limit_bytes=64 * 1024 * 1024),
    )(*results)
    return (across(new)[None], across(grad_feats)[None], g_in, g_out, g_rad)


def solution(mesh):
    return jax.shard_map(
        functools.partial(body, mesh.shape["dp"] // 2, mesh.shape["graph"]),
        mesh=mesh,
        in_specs=(
            P(("groups", "dp"), "graph", None, None),
            P(("groups", "dp"), None, "graph"),
            P(("groups", "dp"), None, None),
            P(("groups", "dp"), "graph"),
            P(("groups", "dp"), "graph"),
            P(("groups", "dp"), "graph"),
            P(("groups", "dp"), None, "graph"),
            P(("groups", "dp"), "graph", None, None),
            P("dp", None),
            P("dp", None),
            P("dp", None),
        ),
        out_specs=(
            P(("groups", "dp"), "graph", None, None),
            P(("groups", "dp"), "graph", None, None),
            P(("groups", "dp"), None),
            P(("groups", "dp"), None),
            P(("groups", "dp"), None),
        ),
        check_vma=False,
    )
```

```python
import functools
import math

import jax
import jax.numpy as jnp
from jax import lax
from jax.experimental import pallas as pl
from jax.experimental.pallas import tpu as pltpu
from jax.sharding import PartitionSpec as P

RB = 128
RIM = 16
EDGE_ROWS = 16
CUTOFF = 48.0
ROOT_THREE = math.sqrt(3.0)
ROOT_FIVE = math.sqrt(5.0)
ROOT_FIFTEEN = math.sqrt(15.0)
MESH = pl.DeviceIdType.MESH
F32 = jnp.float32
BF16 = jnp.bfloat16


def dot(a, b, dims=((1,), (0,))):
    return lax.dot_general(a, b, (dims, ((), ())), preferred_element_type=F32)


def log2(value):
    bits = value.bit_length() - 1
    assert 1 << bits == value
    return bits


class Reduction:
    def __init__(self, place, bufs, sems, out_ref):
        self.place = place
        self.part, self.ra, self.sb, self.rb, self.sc, self.rc, self.rd = bufs
        self.a_s, self.a_r, self.b_s, self.b_r, self.c_s, self.c_r, self.d_s, self.d_r = sems
        self.out_ref = out_ref
        self.sends = []
        self.split = self.rd.shape[1] != self.out_ref.shape[0]

    def send(self, src, dst, send_sem, recv_sem, where):
        copy = pltpu.make_async_remote_copy(
            src_ref=src, dst_ref=dst, send_sem=send_sem, recv_sem=recv_sem,
            device_id=where, device_id_type=MESH,
        )
        copy.start()
        self.sends.append(copy)

    def arrived(self, dst, send_sem, recv_sem, where):
        pltpu.make_async_remote_copy(
            src_ref=dst, dst_ref=dst, send_sem=send_sem, recv_sem=recv_sem,
            device_id=where, device_id_type=MESH,
        ).wait_recv()

    def put(self, value):
        x_count, n = self.part.shape[1], self.part.shape[2]
        for r in range(2 * x_count):
            self.part[r % 2, r // 2] = value[r * n : (r + 1) * n].astype(BF16)

    def stage_a(self):
        core, peer = self.place["core"], self.place["peer"]
        self.send(self.part.at[1 - core], self.ra, self.a_s, self.a_r, {"dp": peer})

    def stage_b(self):
        core, peer, x, xs = (self.place[k] for k in ("core", "peer", "x", "x_count"))
        self.arrived(self.ra, self.a_s, self.a_r, {"dp": peer})
        for i in range(xs):
            self.sb[i] = (self.part.at[core, i][...].astype(F32) + self.ra[i].astype(F32)).astype(BF16)
        for j in range(1, xs):
            to = lax.rem(x + j, xs)
            self.send(self.sb.at[to], self.rb.at[x], self.b_s.at[j], self.b_r.at[x], {"dp": 2 * to + core})

    def stage_c(self):
        core, x, xs, z, zs = (self.place[k] for k in ("core", "x", "x_count", "z", "z_count"))
        total = self.sb.at[x][...].astype(F32)
        for j in range(1, xs):
            frm = lax.rem(x + xs - j, xs)
            self.arrived(self.rb.at[frm], self.b_s.at[j], self.b_r.at[frm], {"dp": 2 * frm + core})
            total = total + self.rb.at[frm][...].astype(F32)
        if self.split:
            self.sc[...] = total.astype(BF16).reshape(self.sc.shape)
            for j in range(1, zs):
                to = lax.rem(z + j, zs)
                self.send(self.sc.at[to], self.rc.at[z], self.c_s.at[j], self.c_r.at[z], {"graph": to})
        else:
            self.rd.at[z][...] = total.astype(BF16)
            self.spread()

    def spread(self):
        z, zs = self.place["z"], self.place["z_count"]
        for j in range(1, zs):
            to = lax.rem(z + j, zs)
            self.send(self.rd.at[z], self.rd.at[z], self.d_s.at[j], self.d_r.at[z], {"graph": to})

    def stage_d(self):
        z, zs = self.place["z"], self.place["z_count"]
        if self.split:
            total = self.sc.at[z][...].astype(F32)
            for j in range(1, zs):
                frm = lax.rem(z + zs - j, zs)
                self.arrived(self.rc.at[frm], self.c_s.at[j], self.c_r.at[frm], {"graph": frm})
                total = total + self.rc.at[frm][...].astype(F32)
            self.rd.at[z][...] = total.astype(BF16)
            self.spread()

    def finish(self):
        z, zs = self.place["z"], self.place["z_count"]
        for j in range(1, zs):
            frm = lax.rem(z + zs - j, zs)
            self.arrived(self.rd.at[frm], self.d_s.at[j], self.d_r.at[frm], {"graph": frm})
        if self.split:
            self.out_ref[...] = self.rd[...].astype(F32).reshape(self.out_ref.shape)
        else:
            total = self.rd[0].astype(F32)
            for i in range(1, zs):
                total = total + self.rd[i].astype(F32)
            self.out_ref[...] = total


def kernel(
    x_count, z_count,
    feat_ref, cot_hbm, frac_hbm, lattice_hbm, count_hbm, target_hbm, source_hbm, shift_hbm,
    win_ref, wout_ref, wrad_ref,
    new_hbm, gf_hbm, gin_hbm, gout_hbm, grad_hbm,
    new_ref, gf_ref, gin_ref, gout_ref, grad_ref, full_in, full_out, full_rad, feat_pad, frac_pad, proj, rows_e, msg_e, dmsg_e, gates, dgates,
    table, columns, basis_l, basis_r, pre, summed_s, dpre_s, dsum_s, d_pad, rim_lo, rim_hi, dproj_s,
    cot_ref, frac_ref, frac_l, frac_r, lattice_ref, count_ref, target_ref, source_ref, shift_ref,
    w_send, w_recv, h_send, h_recv, load_sem, store_sem, *red_scratch,
):
    comps, atoms, channels = feat_ref.shape
    edges = target_ref.shape[1]
    padded = atoms + 2 * RIM
    z = lax.axis_index("graph")
    d = lax.axis_index("dp")
    x, core = lax.div(d, 2), lax.rem(d, 2)
    peer = 2 * x + 1 - core
    place = dict(core=core, peer=peer, x=x, x_count=x_count, z=z, z_count=z_count)
    sends = []
    loads = [
        pltpu.make_async_copy(src, dst, load_sem.at[i])
        for i, (src, dst) in enumerate(
            (
                (feat_ref, feat_pad.at[:, RIM : RIM + atoms]),
                (win_ref, full_in.at[d]),
                (wout_ref, full_out.at[d]),
                (cot_hbm, cot_ref),
                (frac_hbm, frac_ref),
                (lattice_hbm, lattice_ref),
                (count_hbm, count_ref),
                (target_hbm, target_ref),
                (source_hbm, source_ref),
                (shift_hbm, shift_ref),
            )
        )
    ]
    rad_count, rad_wide = wrad_ref.shape
    pieces = rad_wide // full_rad.shape[2]
    rad_loads = [
        pltpu.make_async_copy(
            wrad_ref.at[:, i * rad_wide // pieces : (i + 1) * rad_wide // pieces],
            full_rad.at[d, i * rad_count : (i + 1) * rad_count],
            load_sem.at[10 + i],
        )
        for i in range(pieces)
    ]
    for load in loads[4:] + rad_loads + loads[:4]:
        load.start()

    barrier = pltpu.get_barrier_semaphore()
    for j in range(1, z_count):
        pl.semaphore_signal(barrier, inc=1, device_id={"graph": lax.rem(z + j, z_count)}, device_id_type=MESH)
    for j in range(1, x_count):
        pl.semaphore_signal(
            barrier, inc=1, device_id={"dp": 2 * lax.rem(x + j, x_count) + core}, device_id_type=MESH
        )
    pl.semaphore_signal(barrier, inc=1, device_id={"dp": peer}, device_id_type=MESH)
    pl.semaphore_wait(barrier, z_count - 1 + x_count)

    def remote(src, dst, send_sem, recv_sem, where):
        return pltpu.make_async_remote_copy(
            src_ref=src, dst_ref=dst, send_sem=send_sem, recv_sem=recv_sem,
            device_id=where, device_id_type=MESH,
        )

    def send(*args):
        copy = remote(*args)
        copy.start()
        sends.append(copy)

    def gather_start(i, w_ref, full):
        for j in range(1, x_count):
            to = 2 * lax.rem(x + j, x_count) + core
            send(w_ref, full.at[d], w_send.at[i, j], w_recv.at[i, d], {"dp": to})
        send(w_ref, full.at[d], w_send.at[i, 0], w_recv.at[i, d], {"dp": peer})

    def gather_forward(i, full):
        for j in range(1, x_count):
            frm = 2 * lax.rem(x + x_count - j, x_count) + core
            remote(full.at[frm], full.at[frm], w_send.at[i, j], w_recv.at[i, frm], {"dp": frm}).wait_recv()
            send(full.at[frm], full.at[frm], w_send.at[i, x_count + j - 1], w_recv.at[i, frm], {"dp": peer})

    def gather_finish(i, full):
        for j in range(x_count):
            frm = 2 * lax.rem(x + x_count - j, x_count) + 1 - core
            remote(full.at[frm], full.at[frm], w_send.at[i, 0], w_recv.at[i, frm], {"dp": peer}).wait_recv()

    right = {"graph": lax.rem(z + 1, z_count)}
    left = {"graph": lax.rem(z + z_count - 1, z_count)}
    last = atoms - RIM
    ahead = RIM + atoms
    send(frac_hbm, frac_l, h_send.at[0], h_recv.at[0], right)
    send(frac_hbm, frac_r, h_send.at[1], h_recv.at[1], left)
    gather_start(0, win_ref, full_in)
    send(feat_ref.at[:, last:atoms], feat_pad.at[:, 0:RIM], h_send.at[2], h_recv.at[2], right)
    send(feat_ref.at[:, 0:RIM], feat_pad.at[:, ahead:padded], h_send.at[3], h_recv.at[3], left)
    for load in rad_loads:
        load.wait()
    gather_start(1, full_rad.at[d], full_rad)
    gather_start(2, wout_ref, full_out)

    for load in loads[4:]:
        load.wait()
    remote(frac_l, frac_l, h_send.at[0], h_recv.at[0], left).wait_recv()
    remote(frac_r, frac_r, h_send.at[1], h_recv.at[1], right).wait_recv()
    table[...] = jnp.zeros_like(table)
    for i in range(3):
        table[i : i + 1, 0:RIM] = frac_l[i, :, last:atoms]
        table[i : i + 1, RIM:ahead] = frac_ref[i]
        table[i : i + 1, ahead:padded] = frac_r[i, :, 0:RIM]
    frac_pad[...] = table[:, 0:128].T

    tgt_row = target_ref[...].astype(F32)
    total_atoms = z_count * atoms
    local = source_ref[...] - z * atoms + RIM
    local = jnp.where(local < 0, local + total_atoms, local)
    local = jnp.where(local >= total_atoms, local - total_atoms, local)
    src_row = local.astype(F32)
    live = lax.broadcasted_iota(jnp.int32, (1, edges), 1) < count_ref[...]
    live = jnp.where(live, 1.0, 0.0)
    hot_src_t = lax.broadcasted_iota(jnp.int32, (padded, edges), 0).astype(F32) == src_row
    hot_tgt_t = lax.broadcasted_iota(jnp.int32, (atoms, edges), 0).astype(F32) == tgt_row
    diffs = []
    for i in range(3):
        f_src = jnp.sum(jnp.where(hot_src_t, frac_pad[0:padded, i : i + 1], 0.0), axis=0, keepdims=True)
        f_tgt = jnp.sum(jnp.where(hot_tgt_t, frac_pad[RIM:ahead, i : i + 1], 0.0), axis=0, keepdims=True)
        diffs.append(f_src + shift_ref[i].astype(F32) - f_tgt)
    displace = [
        sum(diffs[i] * lattice_ref[i, :, j : j + 1] for i in range(3)) for j in range(3)
    ]
    distance = jnp.sqrt(
        displace[0] * displace[0] + displace[1] * displace[1] + displace[2] * displace[2] + 1.0
    )
    ux, uy, uz = (displace[j] / distance for j in range(3))
    envelope = 0.5 * (jnp.cos(math.pi * distance / CUTOFF) + 1.0) * live
    entries = [
        envelope,
        ROOT_THREE * uy,
        ROOT_THREE * uz,
        ROOT_THREE * ux,
        ROOT_FIFTEEN * ux * uy,
        ROOT_FIFTEEN * uy * uz,
        0.5 * ROOT_FIVE * (2.0 * uz * uz - ux * ux - uy * uy),
        ROOT_FIFTEEN * ux * uz,
        0.5 * ROOT_FIFTEEN * (ux * ux - uy * uy),
        distance,
        tgt_row,
        src_row,
    ]
    for i, entry in enumerate(entries):
        table[i : i + 1, :] = entry
    columns[...] = table[...].T
    hot_src = (
        lax.broadcasted_iota(jnp.int32, (edges, padded), 1).astype(F32) == columns[:, 11:12]
    ).astype(BF16)
    hot_tgt = (
        lax.broadcasted_iota(jnp.int32, (edges, atoms), 1).astype(F32) == columns[:, 10:11]
    ).astype(BF16)
    hot_src_t = hot_src_t.astype(BF16)
    hot_tgt_t = hot_tgt_t.astype(BF16)

    ranks, rad_rows, rad_cols = full_rad.shape
    quarter = rad_rows // 2
    slot = lax.broadcasted_iota(jnp.int32, (1, 2 * RB), 1)
    half = (slot >> log2(quarter)) & 1
    index = ((slot >> log2(rad_rows)) << log2(quarter)) + (slot & (quarter - 1))
    centres = CUTOFF * index.astype(F32) / (RB - 1)
    offset = (columns[:, 9:10] - centres) / (2.0 * CUTOFF / RB)
    basis = jnp.exp(-(offset * offset)) * columns[:, 0:1]
    basis_l[...] = jnp.where(half == 0, basis, 0.0).astype(BF16)
    basis_r[...] = jnp.where(half == 1, basis, 0.0).astype(BF16)

    for load in loads[:2]:
        load.wait()
    gather_forward(0, full_in)
    gather_forward(1, full_rad)
    gather_finish(1, full_rad)
    rad = full_rad[...].reshape(ranks * rad_rows, rad_cols)
    gates[:, :rad_cols] = dot(basis_l[...], rad)
    gates[:, rad_cols:] = dot(basis_r[...], rad)
    gather_finish(0, full_in)
    remote(feat_pad.at[:, 0:RIM], feat_pad.at[:, 0:RIM], h_send.at[2], h_recv.at[2], left).wait_recv()
    remote(feat_pad.at[:, ahead:padded], feat_pad.at[:, ahead:padded], h_send.at[3], h_recv.at[3], right).wait_recv()
    proj[...] = (
        dot(feat_pad[...].reshape(comps * padded, channels), full_in[...].reshape(channels, channels))
        .astype(BF16)
        .reshape(comps, padded, channels)
    )
    for k in range(comps):
        rows_e[k] = dot(hot_src, proj[k]).astype(BF16)
    for load in loads[2:4]:
        load.wait()
    gather_forward(2, full_out)

    def gate_of(rows):
        return [gates[rows, i * channels : (i + 1) * channels] for i in range(3)]

    @pl.loop(0, edges // EDGE_ROWS)
    def _(step):
        rows = pl.ds(pl.multiple_of(step * EDGE_ROWS, EDGE_ROWS), EDGE_ROWS)
        harm = columns[rows, :]
        g0, g1, g2 = gate_of(rows)
        scalars = rows_e[0, rows, :].astype(F32)
        msg_e[0, rows, :] = (g0 * scalars).astype(BF16)
        for k in range(1, comps):
            inner = harm[:, k : k + 1] * scalars + rows_e[k, rows, :].astype(F32)
            msg_e[k, rows, :] = ((g1 if k < 4 else g2) * inner).astype(BF16)

    for k in range(comps):
        summed_s[k] = (0.25 * dot(hot_tgt_t, msg_e[k])).astype(BF16)
    gather_finish(2, full_out)
    w_out = full_out[...].reshape(channels, channels)
    flat = (comps * atoms, channels)
    pre[...] = dot(summed_s[...].reshape(flat), w_out).reshape(comps, atoms, channels)

    @pl.loop(0, atoms // 16)
    def _(step):
        rows = pl.ds(pl.multiple_of(step * 16, 16), 16)
        shifted = pl.ds(pl.multiple_of(step * 16 + RIM, 16), 16)
        p0 = pre[0, rows, :]
        gate = jax.nn.sigmoid(p0)
        total = jnp.zeros_like(gate)
        for k in range(comps):
            p = pre[k, rows, :]
            u = cot_ref[k, rows, :].astype(F32)
            total = total + u * p
            new_ref[k, rows, :] = (feat_pad[k, shifted, :].astype(F32) + p * gate).astype(BF16)
            if k:
                dpre_s[k, rows, :] = (u * gate).astype(BF16)
        u0 = cot_ref[0, rows, :].astype(F32)
        dpre_s[0, rows, :] = (u0 * gate + gate * (1.0 - gate) * total).astype(BF16)

    stores = []

    def store(i, src, dst):
        copy = pltpu.make_async_copy(src, dst, store_sem.at[i])
        copy.start()
        stores.append(copy)

    store(0, new_ref, new_hbm)
    scale = 1.0 / (z_count * atoms)
    count = len(red_scratch) // 3
    reds = [
        Reduction(place, red_scratch[i * count : i * count + 7], red_scratch[i * count + 7 : (i + 1) * count], out)
        for i, out in enumerate((gout_ref, grad_ref, gin_ref))
    ]
    red_out, red_rad, red_in = reds
    across = ((0,), (0,))
    red_out.put(scale * dot(summed_s[...].reshape(flat), dpre_s[...].reshape(flat), across))
    red_out.stage_a()
    dsum_s[...] = (
        (0.25 * dot(dpre_s[...].reshape(flat), w_out, ((1,), (1,)))).astype(BF16).reshape(comps, atoms, channels)
    )
    for k in range(comps):
        dmsg_e[k] = dot(hot_tgt, dsum_s[k]).astype(BF16)

    @pl.loop(0, edges // EDGE_ROWS)
    def _(step):
        rows = pl.ds(pl.multiple_of(step * EDGE_ROWS, EDGE_ROWS), EDGE_ROWS)
        harm = columns[rows, :]
        g0, g1, g2 = gate_of(rows)
        scalars = rows_e[0, rows, :].astype(F32)
        d0 = dmsg_e[0, rows, :].astype(F32)
        dgates[rows, 0:channels] = (d0 * scalars).astype(BF16)
        d_scalars = d0 * g0
        for lo, hi, gate in ((1, 4, g1), (4, 9, g2)):
            mixed = jnp.zeros_like(d0)
            plain = jnp.zeros_like(d0)
            for k in range(lo, hi):
                dk = dmsg_e[k, rows, :].astype(F32)
                mixed = mixed + dk * harm[:, k : k + 1]
                plain = plain + dk * rows_e[k, rows, :].astype(F32)
                msg_e[k, rows, :] = (gate * dk).astype(BF16)
            block = 1 if lo == 1 else 2
            dgates[rows, block * channels : (block + 1) * channels] = (mixed * scalars + plain).astype(BF16)
            d_scalars = d_scalars + gate * mixed
        msg_e[0, rows, :] = d_scalars.astype(BF16)

    red_out.stage_b()
    for k in range(comps):
        d_pad[k] = dot(hot_src_t, msg_e[k]).astype(BF16)
    send(d_pad.at[:, 0:RIM], rim_hi, h_send.at[4], h_recv.at[4], left)
    send(d_pad.at[:, ahead:padded], rim_lo, h_send.at[5], h_recv.at[5], right)
    red_rad.put(
        scale
        * (
            dot(basis_l[...], dgates[:, :rad_cols], across)
            + dot(basis_r[...], dgates[:, rad_cols:], across)
        )
    )
    red_rad.stage_a()
    red_in.put(
        scale
        * dot(
            feat_pad[...].reshape(comps * padded, channels),
            d_pad[...].reshape(comps * padded, channels),
            across,
        )
    )
    red_in.stage_a()
    red_rad.stage_b()
    red_out.stage_c()
    red_in.stage_b()
    red_rad.stage_c()
    red_out.stage_d()
    red_in.stage_c()
    red_rad.stage_d()
    remote(rim_hi, rim_hi, h_send.at[4], h_recv.at[4], right).wait_recv()
    remote(rim_lo, rim_lo, h_send.at[5], h_recv.at[5], left).wait_recv()
    dproj_s[...] = d_pad[:, RIM:ahead, :]
    dproj_s[:, 0:RIM, :] = (dproj_s[:, 0:RIM, :].astype(F32) + rim_lo[...].astype(F32)).astype(BF16)
    dproj_s[:, last:atoms, :] = (dproj_s[:, last:atoms, :].astype(F32) + rim_hi[...].astype(F32)).astype(BF16)
    back = dot(dproj_s[...].reshape(flat), full_in[...].reshape(channels, channels), ((1,), (1,)))
    gf_ref[...] = (
        (cot_ref[...].reshape(flat).astype(F32) + back).astype(BF16).reshape(comps, atoms, channels)
    )
    store(1, gf_ref, gf_hbm)
    red_in.stage_d()
    red_out.finish()
    store(2, gout_ref, gout_hbm)
    red_rad.finish()
    for i in range(2):
        store(
            3 + i,
            grad_ref.at[i * quarter : (i + 1) * quarter],
            grad_hbm.at[:, i * rad_cols : (i + 1) * rad_cols],
        )
    red_in.finish()
    store(5, gin_ref, gin_hbm)
    for copy in stores:
        copy.wait()
    for red in reds:
        for copy in red.sends:
            copy.wait_send()
    for copy in sends:
        copy.wait_send()


def hand_over(*refs):
    sources, results, held = refs[:5], refs[5:10], refs[10:15]
    sem = refs[15]
    loads = [pltpu.make_async_copy(sources[i], held[i], sem.at[0, i]) for i in range(5)]
    stores = [pltpu.make_async_copy(held[i], results[i], sem.at[1, i]) for i in range(5)]
    for load in loads:
        load.start()
    for load, store in zip(loads, stores):
        load.wait()
        store.start()
    for store in stores:
        store.wait()


def body(x_count, z_count, node_feats, frac_pos, lattice, edge_count, edge_target, edge_source,
         edge_shift, cotangent, w_in, w_out, w_rad):
    atoms, comps, channels = node_feats.shape[1:]
    edges = edge_target.shape[1]
    padded = atoms + 2 * RIM
    dp = 2 * x_count
    across = lambda array: jnp.transpose(array, (1, 0, 2))
    feats = jnp.transpose(node_feats[0], (1, 0, 2))
    cot = jnp.transpose(cotangent[0], (1, 0, 2))
    rad_cols = w_rad.shape[1] // 2
    rows, rad_rows = w_in.shape[0], 2 * w_rad.shape[0]
    rad = w_rad
    if w_rad.shape[0] % 16:
        rad = jnp.concatenate([w_rad[:, :rad_cols], w_rad[:, rad_cols:]], axis=0)

    vmem = lambda shape, dtype=BF16: pltpu.VMEM(shape, dtype)
    dma = pltpu.SemaphoreType.DMA
    scratch = [
        vmem((comps, atoms, channels)), vmem((comps, atoms, channels)), vmem((rows, channels), F32),
        vmem((rows, channels), F32), vmem((rad_rows, rad_cols), F32),
        vmem((dp, rows, channels)), vmem((dp, rows, channels)), vmem((dp, rad_rows, rad_cols)),
        vmem((comps, padded, channels)), vmem((128, 128), F32), vmem((comps, padded, channels)),
        vmem((comps, edges, channels)), vmem((comps, edges, channels)), vmem((comps, edges, channels)),
        vmem((edges, 3 * channels), F32), vmem((edges, 3 * channels)),
        vmem((128, edges), F32), vmem((edges, 128), F32), vmem((edges, 2 * RB)), vmem((edges, 2 * RB)),
        vmem((comps, atoms, channels), F32), vmem((comps, atoms, channels)),
        vmem((comps, atoms, channels)), vmem((comps, atoms, channels)),
        vmem((comps, padded, channels)), vmem((comps, RIM, channels)), vmem((comps, RIM, channels)),
        vmem((comps, atoms, channels)),
        vmem((comps, atoms, channels)), vmem((3, 1, atoms), F32), vmem((3, 1, atoms), F32), vmem((3, 1, atoms), F32),
        vmem((3, 1, 3), F32), vmem((1, 1), jnp.int32), vmem((1, edges), jnp.int32),
        vmem((1, edges), jnp.int32), vmem((3, 1, edges), jnp.int32),
        dma((3, 2 * x_count)), dma((3, dp)), dma((6,)), dma((6,)), dma((12,)), dma((6,)),
    ]
    for n, cols in ((rows, channels), (rad_rows, rad_cols), (rows, channels)):
        piece = n // z_count if n % (16 * z_count) == 0 else n
        scratch += [
            vmem((2, x_count, n, cols)), vmem((x_count, n, cols)), vmem((x_count, n, cols)),
            vmem((x_count, n, cols)), vmem((n // piece, piece, cols)), vmem((z_count, piece, cols)),
            vmem((z_count, piece, cols)),
            dma, dma, dma((x_count,)), dma((x_count,)), dma((z_count,)), dma((z_count,)),
            dma((z_count,)), dma((z_count,)),
        ]
    outs = [
        jax.ShapeDtypeStruct((comps, atoms, channels), BF16),
        jax.ShapeDtypeStruct((comps, atoms, channels), BF16),
        jax.ShapeDtypeStruct((rows, channels), F32),
        jax.ShapeDtypeStruct((rows, channels), F32),
        jax.ShapeDtypeStruct((rad_rows // 2, 2 * rad_cols), F32),
    ]
    results = pl.pallas_call(
        functools.partial(kernel, x_count, z_count),
        out_shape=outs,
        in_specs=[pl.BlockSpec(memory_space=pltpu.HBM)] * 11,
        out_specs=[pl.BlockSpec(memory_space=pltpu.HBM)] * 5,
        scratch_shapes=scratch,
        compiler_params=pltpu.CompilerParams(
            collective_id=0, has_side_effects=True, vmem_limit_bytes=64 * 1024 * 1024
        ),
    )(
        feats, cot, across(frac_pos), across(lattice), edge_count, edge_target, edge_source, across(edge_shift),
        w_in, w_out, rad,
    )
    new, grad_feats, g_in, g_out, g_rad = pl.pallas_call(
        hand_over,
        out_shape=outs,
        in_specs=[pl.BlockSpec(memory_space=pltpu.HBM)] * 5,
        out_specs=[pl.BlockSpec(memory_space=pltpu.HBM)] * 5,
        scratch_shapes=[vmem(out.shape, out.dtype) for out in outs] + [dma((2, 5))],
        compiler_params=pltpu.CompilerParams(vmem_limit_bytes=64 * 1024 * 1024),
    )(*results)
    return (across(new)[None], across(grad_feats)[None], g_in, g_out, g_rad)


def solution(mesh):
    return jax.shard_map(
        functools.partial(body, mesh.shape["dp"] // 2, mesh.shape["graph"]),
        mesh=mesh,
        in_specs=(
            P(("groups", "dp"), "graph", None, None),
            P(("groups", "dp"), None, "graph"),
            P(("groups", "dp"), None, None),
            P(("groups", "dp"), "graph"),
            P(("groups", "dp"), "graph"),
            P(("groups", "dp"), "graph"),
            P(("groups", "dp"), None, "graph"),
            P(("groups", "dp"), "graph", None, None),
            P("dp", None),
            P("dp", None),
            P("dp", None),
        ),
        out_specs=(
            P(("groups", "dp"), "graph", None, None),
            P(("groups", "dp"), "graph", None, None),
            P(("groups", "dp"), None),
            P(("groups", "dp"), None),
            P(("groups", "dp"), None),
        ),
        check_vma=False,
    )
```

```python
import functools
import math

import jax
import jax.numpy as jnp
from jax import lax
from jax.experimental import pallas as pl
from jax.experimental.pallas import tpu as pltpu
from jax.sharding import PartitionSpec as P

RB = 128
RIM = 16
EDGE_ROWS = 16
CUTOFF = 48.0
ROOT_THREE = math.sqrt(3.0)
ROOT_FIVE = math.sqrt(5.0)
ROOT_FIFTEEN = math.sqrt(15.0)
MESH = pl.DeviceIdType.MESH
F32 = jnp.float32
BF16 = jnp.bfloat16


def dot(a, b, dims=((1,), (0,))):
    return lax.dot_general(a, b, (dims, ((), ())), preferred_element_type=F32)


def log2(value):
    bits = value.bit_length() - 1
    assert 1 << bits == value
    return bits


class Reduction:
    def __init__(self, place, bufs, sems, out_ref):
        self.place = place
        self.part, self.ra, self.sb, self.rb, self.sc, self.rc, self.rd = bufs
        self.a_s, self.a_r, self.b_s, self.b_r, self.c_s, self.c_r, self.d_s, self.d_r = sems
        self.out_ref = out_ref
        self.sends = []
        self.split = self.rd.shape[1] != self.out_ref.shape[0]

    def send(self, src, dst, send_sem, recv_sem, where):
        copy = pltpu.make_async_remote_copy(
            src_ref=src, dst_ref=dst, send_sem=send_sem, recv_sem=recv_sem,
            device_id=where, device_id_type=MESH,
        )
        copy.start()
        self.sends.append(copy)

    def arrived(self, dst, send_sem, recv_sem, where):
        pltpu.make_async_remote_copy(
            src_ref=dst, dst_ref=dst, send_sem=send_sem, recv_sem=recv_sem,
            device_id=where, device_id_type=MESH,
        ).wait_recv()

    def put(self, value):
        x_count, n = self.part.shape[1], self.part.shape[2]
        for r in range(2 * x_count):
            self.part[r % 2, r // 2] = value[r * n : (r + 1) * n].astype(BF16)

    def stage_a(self):
        core, peer = self.place["core"], self.place["peer"]
        self.send(self.part.at[1 - core], self.ra, self.a_s, self.a_r, {"dp": peer})

    def stage_b(self):
        core, peer, x, xs = (self.place[k] for k in ("core", "peer", "x", "x_count"))
        self.arrived(self.ra, self.a_s, self.a_r, {"dp": peer})
        for i in range(xs):
            self.sb[i] = (self.part.at[core, i][...].astype(F32) + self.ra[i].astype(F32)).astype(BF16)
        for j in range(1, xs):
            to = lax.rem(x + j, xs)
            self.send(self.sb.at[to], self.rb.at[x], self.b_s.at[j], self.b_r.at[x], {"dp": 2 * to + core})

    def stage_c(self):
        core, x, xs, z, zs = (self.place[k] for k in ("core", "x", "x_count", "z", "z_count"))
        total = self.sb.at[x][...].astype(F32)
        for j in range(1, xs):
            frm = lax.rem(x + xs - j, xs)
            self.arrived(self.rb.at[frm], self.b_s.at[j], self.b_r.at[frm], {"dp": 2 * frm + core})
            total = total + self.rb.at[frm][...].astype(F32)
        if self.split:
            self.sc[...] = total.astype(BF16).reshape(self.sc.shape)
            for j in range(1, zs):
                to = lax.rem(z + j, zs)
                self.send(self.sc.at[to], self.rc.at[z], self.c_s.at[j], self.c_r.at[z], {"graph": to})
        else:
            self.rd.at[z][...] = total.astype(BF16)
            self.spread()

    def spread(self):
        z, zs = self.place["z"], self.place["z_count"]
        for j in range(1, zs):
            to = lax.rem(z + j, zs)
            self.send(self.rd.at[z], self.rd.at[z], self.d_s.at[j], self.d_r.at[z], {"graph": to})

    def stage_d(self):
        z, zs = self.place["z"], self.place["z_count"]
        if self.split:
            total = self.sc.at[z][...].astype(F32)
            for j in range(1, zs):
                frm = lax.rem(z + zs - j, zs)
                self.arrived(self.rc.at[frm], self.c_s.at[j], self.c_r.at[frm], {"graph": frm})
                total = total + self.rc.at[frm][...].astype(F32)
            self.rd.at[z][...] = total.astype(BF16)
            self.spread()

    def finish(self):
        z, zs = self.place["z"], self.place["z_count"]
        for j in range(1, zs):
            frm = lax.rem(z + zs - j, zs)
            self.arrived(self.rd.at[frm], self.d_s.at[j], self.d_r.at[frm], {"graph": frm})
        if self.split:
            self.out_ref[...] = self.rd[...].astype(F32).reshape(self.out_ref.shape)
        else:
            total = self.rd[0].astype(F32)
            for i in range(1, zs):
                total = total + self.rd[i].astype(F32)
            self.out_ref[...] = total


def kernel(
    x_count, z_count,
    feat_ref, cot_hbm, frac_hbm, lattice_hbm, count_hbm, target_hbm, source_hbm, shift_hbm,
    win_ref, wout_ref, wrad_ref,
    new_hbm, gf_hbm, gin_hbm, gout_hbm, grad_hbm,
    new_ref, gf_ref, gin_ref, gout_ref, grad_ref, full_in, full_out, full_rad, feat_pad, frac_pad, proj, rows_e, msg_e, dmsg_e, gates, dgates,
    table, columns, basis_l, basis_r, pre, summed_s, dpre_s, dsum_s, d_pad, rim_lo, rim_hi, dproj_s,
    cot_ref, frac_ref, frac_l, frac_r, lattice_ref, count_ref, target_ref, source_ref, shift_ref,
    w_send, w_recv, h_send, h_recv, load_sem, store_sem, *red_scratch,
):
    comps, atoms, channels = feat_ref.shape
    edges = target_ref.shape[1]
    padded = atoms + 2 * RIM
    z = lax.axis_index("graph")
    d = lax.axis_index("dp")
    x, core = lax.div(d, 2), lax.rem(d, 2)
    peer = 2 * x + 1 - core
    place = dict(core=core, peer=peer, x=x, x_count=x_count, z=z, z_count=z_count)
    sends = []
    loads = [
        pltpu.make_async_copy(src, dst, load_sem.at[i])
        for i, (src, dst) in enumerate(
            (
                (feat_ref, feat_pad.at[:, RIM : RIM + atoms]),
                (win_ref, full_in.at[d]),
                (wout_ref, full_out.at[d]),
                (cot_hbm, cot_ref),
                (frac_hbm, frac_ref),
                (lattice_hbm, lattice_ref),
                (count_hbm, count_ref),
                (target_hbm, target_ref),
                (source_hbm, source_ref),
                (shift_hbm, shift_ref),
            )
        )
    ]
    rad_count, rad_wide = wrad_ref.shape
    pieces = rad_wide // full_rad.shape[2]
    rad_loads = [
        pltpu.make_async_copy(
            wrad_ref.at[:, i * rad_wide // pieces : (i + 1) * rad_wide // pieces],
            full_rad.at[d, i * rad_count : (i + 1) * rad_count],
            load_sem.at[10 + i],
        )
        for i in range(pieces)
    ]
    for load in loads[4:] + rad_loads + loads[:4]:
        load.start()

    barrier = pltpu.get_barrier_semaphore()
    for j in range(1, z_count):
        pl.semaphore_signal(barrier, inc=1, device_id={"graph": lax.rem(z + j, z_count)}, device_id_type=MESH)
    for j in range(1, x_count):
        pl.semaphore_signal(
            barrier, inc=1, device_id={"dp": 2 * lax.rem(x + j, x_count) + core}, device_id_type=MESH
        )
    pl.semaphore_signal(barrier, inc=1, device_id={"dp": peer}, device_id_type=MESH)
    pl.semaphore_wait(barrier, z_count - 1 + x_count)

    def remote(src, dst, send_sem, recv_sem, where):
        return pltpu.make_async_remote_copy(
            src_ref=src, dst_ref=dst, send_sem=send_sem, recv_sem=recv_sem,
            device_id=where, device_id_type=MESH,
        )

    def send(*args):
        copy = remote(*args)
        copy.start()
        sends.append(copy)

    def gather_start(i, w_ref, full):
        for j in range(1, x_count):
            to = 2 * lax.rem(x + j, x_count) + core
            send(w_ref, full.at[d], w_send.at[i, j], w_recv.at[i, d], {"dp": to})
        send(w_ref, full.at[d], w_send.at[i, 0], w_recv.at[i, d], {"dp": peer})

    def gather_forward(i, full):
        for j in range(1, x_count):
            frm = 2 * lax.rem(x + x_count - j, x_count) + core
            remote(full.at[frm], full.at[frm], w_send.at[i, j], w_recv.at[i, frm], {"dp": frm}).wait_recv()
            send(full.at[frm], full.at[frm], w_send.at[i, x_count + j - 1], w_recv.at[i, frm], {"dp": peer})

    def gather_finish(i, full):
        for j in range(x_count):
            frm = 2 * lax.rem(x + x_count - j, x_count) + 1 - core
            remote(full.at[frm], full.at[frm], w_send.at[i, 0], w_recv.at[i, frm], {"dp": peer}).wait_recv()

    right = {"graph": lax.rem(z + 1, z_count)}
    left = {"graph": lax.rem(z + z_count - 1, z_count)}
    last = atoms - RIM
    ahead = RIM + atoms
    send(frac_hbm, frac_l, h_send.at[0], h_recv.at[0], right)
    send(frac_hbm, frac_r, h_send.at[1], h_recv.at[1], left)
    gather_start(0, win_ref, full_in)
    send(feat_ref.at[:, last:atoms], feat_pad.at[:, 0:RIM], h_send.at[2], h_recv.at[2], right)
    send(feat_ref.at[:, 0:RIM], feat_pad.at[:, ahead:padded], h_send.at[3], h_recv.at[3], left)
    for load in rad_loads:
        load.wait()
    gather_start(1, full_rad.at[d], full_rad)
    gather_start(2, wout_ref, full_out)

    for load in loads[4:]:
        load.wait()
    gather_forward(0, full_in)
    remote(frac_l, frac_l, h_send.at[0], h_recv.at[0], left).wait_recv()
    remote(frac_r, frac_r, h_send.at[1], h_recv.at[1], right).wait_recv()
    table[...] = jnp.zeros_like(table)
    for i in range(3):
        table[i : i + 1, 0:RIM] = frac_l[i, :, last:atoms]
        table[i : i + 1, RIM:ahead] = frac_ref[i]
        table[i : i + 1, ahead:padded] = frac_r[i, :, 0:RIM]
    frac_pad[...] = table[:, 0:128].T

    tgt_row = target_ref[...].astype(F32)
    total_atoms = z_count * atoms
    local = source_ref[...] - z * atoms + RIM
    local = jnp.where(local < 0, local + total_atoms, local)
    local = jnp.where(local >= total_atoms, local - total_atoms, local)
    src_row = local.astype(F32)
    live = lax.broadcasted_iota(jnp.int32, (1, edges), 1) < count_ref[...]
    live = jnp.where(live, 1.0, 0.0)
    hot_src_t = lax.broadcasted_iota(jnp.int32, (padded, edges), 0).astype(F32) == src_row
    hot_tgt_t = lax.broadcasted_iota(jnp.int32, (atoms, edges), 0).astype(F32) == tgt_row
    diffs = []
    for i in range(3):
        f_src = jnp.sum(jnp.where(hot_src_t, frac_pad[0:padded, i : i + 1], 0.0), axis=0, keepdims=True)
        f_tgt = jnp.sum(jnp.where(hot_tgt_t, frac_pad[RIM:ahead, i : i + 1], 0.0), axis=0, keepdims=True)
        diffs.append(f_src + shift_ref[i].astype(F32) - f_tgt)
    displace = [
        sum(diffs[i] * lattice_ref[i, :, j : j + 1] for i in range(3)) for j in range(3)
    ]
    distance = jnp.sqrt(
        displace[0] * displace[0] + displace[1] * displace[1] + displace[2] * displace[2] + 1.0
    )
    ux, uy, uz = (displace[j] / distance for j in range(3))
    envelope = 0.5 * (jnp.cos(math.pi * distance / CUTOFF) + 1.0) * live
    entries = [
        envelope,
        ROOT_THREE * uy,
        ROOT_THREE * uz,
        ROOT_THREE * ux,
        ROOT_FIFTEEN * ux * uy,
        ROOT_FIFTEEN * uy * uz,
        0.5 * ROOT_FIVE * (2.0 * uz * uz - ux * ux - uy * uy),
        ROOT_FIFTEEN * ux * uz,
        0.5 * ROOT_FIFTEEN * (ux * ux - uy * uy),
        distance,
        tgt_row,
        src_row,
    ]
    for i, entry in enumerate(entries):
        table[i : i + 1, :] = entry
    columns[...] = table[...].T
    hot_src = (
        lax.broadcasted_iota(jnp.int32, (edges, padded), 1).astype(F32) == columns[:, 11:12]
    ).astype(BF16)
    hot_tgt = (
        lax.broadcasted_iota(jnp.int32, (edges, atoms), 1).astype(F32) == columns[:, 10:11]
    ).astype(BF16)
    hot_src_t = hot_src_t.astype(BF16)
    hot_tgt_t = hot_tgt_t.astype(BF16)

    gather_forward(1, full_rad)
    ranks, rad_rows, rad_cols = full_rad.shape
    quarter = rad_rows // 2
    slot = lax.broadcasted_iota(jnp.int32, (1, 2 * RB), 1)
    half = (slot >> log2(quarter)) & 1
    index = ((slot >> log2(rad_rows)) << log2(quarter)) + (slot & (quarter - 1))
    centres = CUTOFF * index.astype(F32) / (RB - 1)
    offset = (columns[:, 9:10] - centres) / (2.0 * CUTOFF / RB)
    basis = jnp.exp(-(offset * offset)) * columns[:, 0:1]
    basis_l[...] = jnp.where(half == 0, basis, 0.0).astype(BF16)
    basis_r[...] = jnp.where(half == 1, basis, 0.0).astype(BF16)

    for load in loads[:2]:
        load.wait()
    gather_finish(1, full_rad)
    rad = full_rad[...].reshape(ranks * rad_rows, rad_cols)
    gates[:, :rad_cols] = dot(basis_l[...], rad)
    gates[:, rad_cols:] = dot(basis_r[...], rad)
    gather_finish(0, full_in)
    remote(feat_pad.at[:, 0:RIM], feat_pad.at[:, 0:RIM], h_send.at[2], h_recv.at[2], left).wait_recv()
    remote(feat_pad.at[:, ahead:padded], feat_pad.at[:, ahead:padded], h_send.at[3], h_recv.at[3], right).wait_recv()
    proj[...] = (
        dot(feat_pad[...].reshape(comps * padded, channels), full_in[...].reshape(channels, channels))
        .astype(BF16)
        .reshape(comps, padded, channels)
    )
    for k in range(comps):
        rows_e[k] = dot(hot_src, proj[k]).astype(BF16)
    for load in loads[2:4]:
        load.wait()
    gather_forward(2, full_out)

    def gate_of(rows):
        return [gates[rows, i * channels : (i + 1) * channels] for i in range(3)]

    @pl.loop(0, edges // EDGE_ROWS)
    def _(step):
        rows = pl.ds(pl.multiple_of(step * EDGE_ROWS, EDGE_ROWS), EDGE_ROWS)
        harm = columns[rows, :]
        g0, g1, g2 = gate_of(rows)
        scalars = rows_e[0, rows, :].astype(F32)
        msg_e[0, rows, :] = (g0 * scalars).astype(BF16)
        for k in range(1, comps):
            inner = harm[:, k : k + 1] * scalars + rows_e[k, rows, :].astype(F32)
            msg_e[k, rows, :] = ((g1 if k < 4 else g2) * inner).astype(BF16)

    for k in range(comps):
        summed_s[k] = (0.25 * dot(hot_tgt_t, msg_e[k])).astype(BF16)
    gather_finish(2, full_out)
    w_out = full_out[...].reshape(channels, channels)
    flat = (comps * atoms, channels)
    pre[...] = dot(summed_s[...].reshape(flat), w_out).reshape(comps, atoms, channels)

    @pl.loop(0, atoms // 16)
    def _(step):
        rows = pl.ds(pl.multiple_of(step * 16, 16), 16)
        shifted = pl.ds(pl.multiple_of(step * 16 + RIM, 16), 16)
        p0 = pre[0, rows, :]
        gate = jax.nn.sigmoid(p0)
        total = jnp.zeros_like(gate)
        for k in range(comps):
            p = pre[k, rows, :]
            u = cot_ref[k, rows, :].astype(F32)
            total = total + u * p
            new_ref[k, rows, :] = (feat_pad[k, shifted, :].astype(F32) + p * gate).astype(BF16)
            if k:
                dpre_s[k, rows, :] = (u * gate).astype(BF16)
        u0 = cot_ref[0, rows, :].astype(F32)
        dpre_s[0, rows, :] = (u0 * gate + gate * (1.0 - gate) * total).astype(BF16)

    stores = []

    def store(i, src, dst):
        copy = pltpu.make_async_copy(src, dst, store_sem.at[i])
        copy.start()
        stores.append(copy)

    store(0, new_ref, new_hbm)
    scale = 1.0 / (z_count * atoms)
    count = len(red_scratch) // 3
    reds = [
        Reduction(place, red_scratch[i * count : i * count + 7], red_scratch[i * count + 7 : (i + 1) * count], out)
        for i, out in enumerate((gout_ref, grad_ref, gin_ref))
    ]
    red_out, red_rad, red_in = reds
    across = ((0,), (0,))
    red_out.put(scale * dot(summed_s[...].reshape(flat), dpre_s[...].reshape(flat), across))
    red_out.stage_a()
    dsum_s[...] = (
        (0.25 * dot(dpre_s[...].reshape(flat), w_out, ((1,), (1,)))).astype(BF16).reshape(comps, atoms, channels)
    )
    for k in range(comps):
        dmsg_e[k] = dot(hot_tgt, dsum_s[k]).astype(BF16)

    @pl.loop(0, edges // EDGE_ROWS)
    def _(step):
        rows = pl.ds(pl.multiple_of(step * EDGE_ROWS, EDGE_ROWS), EDGE_ROWS)
        harm = columns[rows, :]
        g0, g1, g2 = gate_of(rows)
        scalars = rows_e[0, rows, :].astype(F32)
        d0 = dmsg_e[0, rows, :].astype(F32)
        dgates[rows, 0:channels] = (d0 * scalars).astype(BF16)
        d_scalars = d0 * g0
        for lo, hi, gate in ((1, 4, g1), (4, 9, g2)):
            mixed = jnp.zeros_like(d0)
            plain = jnp.zeros_like(d0)
            for k in range(lo, hi):
                dk = dmsg_e[k, rows, :].astype(F32)
                mixed = mixed + dk * harm[:, k : k + 1]
                plain = plain + dk * rows_e[k, rows, :].astype(F32)
                msg_e[k, rows, :] = (gate * dk).astype(BF16)
            block = 1 if lo == 1 else 2
            dgates[rows, block * channels : (block + 1) * channels] = (mixed * scalars + plain).astype(BF16)
            d_scalars = d_scalars + gate * mixed
        msg_e[0, rows, :] = d_scalars.astype(BF16)

    red_out.stage_b()
    for k in range(comps):
        d_pad[k] = dot(hot_src_t, msg_e[k]).astype(BF16)
    send(d_pad.at[:, 0:RIM], rim_hi, h_send.at[4], h_recv.at[4], left)
    send(d_pad.at[:, ahead:padded], rim_lo, h_send.at[5], h_recv.at[5], right)
    red_rad.put(
        scale
        * (
            dot(basis_l[...], dgates[:, :rad_cols], across)
            + dot(basis_r[...], dgates[:, rad_cols:], across)
        )
    )
    red_rad.stage_a()
    red_in.put(
        scale
        * dot(
            feat_pad[...].reshape(comps * padded, channels),
            d_pad[...].reshape(comps * padded, channels),
            across,
        )
    )
    red_in.stage_a()
    red_rad.stage_b()
    red_out.stage_c()
    red_in.stage_b()
    red_rad.stage_c()
    red_out.stage_d()
    red_in.stage_c()
    red_rad.stage_d()
    remote(rim_hi, rim_hi, h_send.at[4], h_recv.at[4], right).wait_recv()
    remote(rim_lo, rim_lo, h_send.at[5], h_recv.at[5], left).wait_recv()
    dproj_s[...] = d_pad[:, RIM:ahead, :]
    dproj_s[:, 0:RIM, :] = (dproj_s[:, 0:RIM, :].astype(F32) + rim_lo[...].astype(F32)).astype(BF16)
    dproj_s[:, last:atoms, :] = (dproj_s[:, last:atoms, :].astype(F32) + rim_hi[...].astype(F32)).astype(BF16)
    back = dot(dproj_s[...].reshape(flat), full_in[...].reshape(channels, channels), ((1,), (1,)))
    gf_ref[...] = (
        (cot_ref[...].reshape(flat).astype(F32) + back).astype(BF16).reshape(comps, atoms, channels)
    )
    store(1, gf_ref, gf_hbm)
    red_in.stage_d()
    red_out.finish()
    store(2, gout_ref, gout_hbm)
    red_rad.finish()
    for i in range(2):
        store(
            3 + i,
            grad_ref.at[i * quarter : (i + 1) * quarter],
            grad_hbm.at[:, i * rad_cols : (i + 1) * rad_cols],
        )
    red_in.finish()
    store(5, gin_ref, gin_hbm)
    for copy in stores:
        copy.wait()
    for red in reds:
        for copy in red.sends:
            copy.wait_send()
    for copy in sends:
        copy.wait_send()


def hand_over(*refs):
    sources, results, held = refs[:5], refs[5:10], refs[10:15]
    sem = refs[15]
    loads = [pltpu.make_async_copy(sources[i], held[i], sem.at[0, i]) for i in range(5)]
    stores = [pltpu.make_async_copy(held[i], results[i], sem.at[1, i]) for i in range(5)]
    for load in loads:
        load.start()
    for load, store in zip(loads, stores):
        load.wait()
        store.start()
    for store in stores:
        store.wait()


def body(x_count, z_count, node_feats, frac_pos, lattice, edge_count, edge_target, edge_source,
         edge_shift, cotangent, w_in, w_out, w_rad):
    atoms, comps, channels = node_feats.shape[1:]
    edges = edge_target.shape[1]
    padded = atoms + 2 * RIM
    dp = 2 * x_count
    across = lambda array: jnp.transpose(array, (1, 0, 2))
    feats = jnp.transpose(node_feats[0], (1, 0, 2))
    cot = jnp.transpose(cotangent[0], (1, 0, 2))
    rad_cols = w_rad.shape[1] // 2
    rows, rad_rows = w_in.shape[0], 2 * w_rad.shape[0]
    rad = w_rad
    if w_rad.shape[0] % 16:
        rad = jnp.concatenate([w_rad[:, :rad_cols], w_rad[:, rad_cols:]], axis=0)

    vmem = lambda shape, dtype=BF16: pltpu.VMEM(shape, dtype)
    dma = pltpu.SemaphoreType.DMA
    scratch = [
        vmem((comps, atoms, channels)), vmem((comps, atoms, channels)), vmem((rows, channels), F32),
        vmem((rows, channels), F32), vmem((rad_rows, rad_cols), F32),
        vmem((dp, rows, channels)), vmem((dp, rows, channels)), vmem((dp, rad_rows, rad_cols)),
        vmem((comps, padded, channels)), vmem((128, 128), F32), vmem((comps, padded, channels)),
        vmem((comps, edges, channels)), vmem((comps, edges, channels)), vmem((comps, edges, channels)),
        vmem((edges, 3 * channels), F32), vmem((edges, 3 * channels)),
        vmem((128, edges), F32), vmem((edges, 128), F32), vmem((edges, 2 * RB)), vmem((edges, 2 * RB)),
        vmem((comps, atoms, channels), F32), vmem((comps, atoms, channels)),
        vmem((comps, atoms, channels)), vmem((comps, atoms, channels)),
        vmem((comps, padded, channels)), vmem((comps, RIM, channels)), vmem((comps, RIM, channels)),
        vmem((comps, atoms, channels)),
        vmem((comps, atoms, channels)), vmem((3, 1, atoms), F32), vmem((3, 1, atoms), F32), vmem((3, 1, atoms), F32),
        vmem((3, 1, 3), F32), vmem((1, 1), jnp.int32), vmem((1, edges), jnp.int32),
        vmem((1, edges), jnp.int32), vmem((3, 1, edges), jnp.int32),
        dma((3, 2 * x_count)), dma((3, dp)), dma((6,)), dma((6,)), dma((12,)), dma((6,)),
    ]
    for n, cols in ((rows, channels), (rad_rows, rad_cols), (rows, channels)):
        piece = n // z_count if n % (16 * z_count) == 0 else n
        scratch += [
            vmem((2, x_count, n, cols)), vmem((x_count, n, cols)), vmem((x_count, n, cols)),
            vmem((x_count, n, cols)), vmem((n // piece, piece, cols)), vmem((z_count, piece, cols)),
            vmem((z_count, piece, cols)),
            dma, dma, dma((x_count,)), dma((x_count,)), dma((z_count,)), dma((z_count,)),
            dma((z_count,)), dma((z_count,)),
        ]
    outs = [
        jax.ShapeDtypeStruct((comps, atoms, channels), BF16),
        jax.ShapeDtypeStruct((comps, atoms, channels), BF16),
        jax.ShapeDtypeStruct((rows, channels), F32),
        jax.ShapeDtypeStruct((rows, channels), F32),
        jax.ShapeDtypeStruct((rad_rows // 2, 2 * rad_cols), F32),
    ]
    results = pl.pallas_call(
        functools.partial(kernel, x_count, z_count),
        out_shape=outs,
        in_specs=[pl.BlockSpec(memory_space=pltpu.HBM)] * 11,
        out_specs=[pl.BlockSpec(memory_space=pltpu.HBM)] * 5,
        scratch_shapes=scratch,
        compiler_params=pltpu.CompilerParams(
            collective_id=0, has_side_effects=True, vmem_limit_bytes=64 * 1024 * 1024
        ),
    )(
        feats, cot, across(frac_pos), across(lattice), edge_count, edge_target, edge_source, across(edge_shift),
        w_in, w_out, rad,
    )
    new, grad_feats, g_in, g_out, g_rad = pl.pallas_call(
        hand_over,
        out_shape=outs,
        in_specs=[pl.BlockSpec(memory_space=pltpu.HBM)] * 5,
        out_specs=[pl.BlockSpec(memory_space=pltpu.HBM)] * 5,
        scratch_shapes=[vmem(out.shape, out.dtype) for out in outs] + [dma((2, 5))],
        compiler_params=pltpu.CompilerParams(vmem_limit_bytes=64 * 1024 * 1024),
    )(*results)
    return (across(new)[None], across(grad_feats)[None], g_in, g_out, g_rad)


def solution(mesh):
    return jax.shard_map(
        functools.partial(body, mesh.shape["dp"] // 2, mesh.shape["graph"]),
        mesh=mesh,
        in_specs=(
            P(("groups", "dp"), "graph", None, None),
            P(("groups", "dp"), None, "graph"),
            P(("groups", "dp"), None, None),
            P(("groups", "dp"), "graph"),
            P(("groups", "dp"), "graph"),
            P(("groups", "dp"), "graph"),
            P(("groups", "dp"), None, "graph"),
            P(("groups", "dp"), "graph", None, None),
            P("dp", None),
            P("dp", None),
            P("dp", None),
        ),
        out_specs=(
            P(("groups", "dp"), "graph", None, None),
            P(("groups", "dp"), "graph", None, None),
            P(("groups", "dp"), None),
            P(("groups", "dp"), None),
            P(("groups", "dp"), None),
        ),
        check_vma=False,
    )
```
